32 devices in a mesh: dp: 4 (over y, x), tensor: 8 (over z, core).
Axes of the slice: x: 2, y: 2, z: 4, core: 2. Of those that a mesh axis runs over, the one named last changes fastest.
Arguments:
- tokens: bfloat16 [1024, 2048], P(('dp', 'tensor')), may hold values from -6 to 6
- attn_gain: bfloat16 [2048], replicated, may hold values from 0.099609375 to 1.8984375
- mlp_gain: bfloat16 [2048], replicated, may hold values from 0.099609375 to 1.8984375
- project_in: bfloat16 [3, 2048, 2048], P(None, None, 'tensor'), may hold values from -6 to 6
- project_out: bfloat16 [2048, 2048], P('tensor'), may hold values from -0.125 to 0.125
- gate_up: bfloat16 [2, 2048, 8192], P(None, None, 'tensor'), may hold values from -0.125 to 0.125
- project_down: bfloat16 [8192, 2048], P('tensor'), may hold values from -0.0625 to 0.0625
- kv_cache: bfloat16 [2, 16384, 2048], P(None, 'dp', 'tensor'), may hold values from -10 to 10
- lengths: int32 [1024], replicated, may hold values from 1 to 1024, as said below
- owners: int32 [1024], replicated, may hold values from 0 to 3, as said below
- cache_start: int32 [1024], replicated, may hold values from 0 to 4094, as said below
Outputs:
- hidden_states: bfloat16 [1024, 2048], P(('dp', 'tensor'))
- log_sum_exp: float32 [1024, 32], P('dp', 'tensor')
- kv_updated: bfloat16 [2, 16384, 2048], P(None, 'dp', 'tensor')
The draws below stay inside these ranges and needn't reach their ends.
Inputs may be any that keep to these rules, and one draw needn't show every extreme that they name: `lengths`: the largest length is exactly 1024 in every draw. `owners`: in each aligned block of 256 requests (those of one dp index) exactly 128 requests name another owner than the block's index and the rest name the block's index; no other owner is named by more than 43 requests of one block, and in every block one owner is named by exactly 43. The requests of one owner occupy disjoint ranges of positions from cache_start to cache_start + length, the last of these (the position for the new token) included, all within that owner's 4096 positions.
All inputs are finite; a program needn't handle non-finite values.
Results may differ from the reference program's by a relative error of at most 0.008.
Values may be sent and summed in bfloat16 or wider, within the bound.
No kernel may reach another device: no remote copies, remote signals or barrier semaphores. Data moves between devices by JAX's collectives and lax.ppermute only.
A program may use at most 64 MiB of HBM per device.

```python
import jax
import jax.numpy as jnp
from jax import lax

D = 2048
FF = 8192
HEADS = 32
REQ_DEV = 256
MAXLEN = 1024
HD = 64
REQUESTS = 1024
CAP = 43
ROWS = 4096
CACHE_ROWS = 16384


def layout_ints(key):
    group_count = REQUESTS // REQ_DEV
    remote_count = REQ_DEV // 2
    key_list = jax.random.split(jax.random.fold_in(key, 17), 6)
    shuffled = jax.vmap(lambda sub_key: jax.random.permutation(sub_key, REQ_DEV))(jax.random.split(key_list[0], group_count))
    ranking = jnp.argsort(shuffled, axis=1).astype(jnp.int32)
    hot_offset = jax.random.randint(key_list[1], (group_count, 1), 0, group_count - 1)
    shift_by = jax.random.randint(key_list[2], (group_count, 1), 0, group_count - 2)
    rest_offset = (hot_offset + 1 + (ranking - CAP + shift_by) % (group_count - 2)) % (group_count - 1)
    offsets = jnp.where(ranking < CAP, hot_offset, rest_offset)
    source = jnp.arange(group_count, dtype=jnp.int32)[:, None]
    owners = jnp.where(ranking < remote_count, (source + 1 + offsets) % group_count, source)
    owners = owners.reshape(REQUESTS).astype(jnp.int32)
    onehot = (owners[:, None] == jnp.arange(group_count, dtype=jnp.int32)[None, :]).astype(jnp.int32)
    hosted = jnp.sum(onehot, axis=0)
    before = jnp.cumsum(onehot, axis=0) - onehot
    host_rank = jnp.sum(before * onehot, axis=1)
    weights = jax.random.randint(key_list[3], (REQUESTS,), 1, 9)
    zone_pick = jax.random.randint(key_list[4], (), 0, group_count)
    shares = jax.random.randint(key_list[5], (group_count,), 1, 5)
    shares = jnp.where(jnp.arange(group_count) == zone_pick, 4, shares)
    weights = jnp.where((owners == zone_pick) & (host_rank == 0), 100000, weights)
    total_weight = jnp.sum(onehot * weights[:, None], axis=0)
    budget = (ROWS - 2 * hosted) * shares // 4
    lengths = jnp.minimum(MAXLEN, 1 + weights * jnp.take(budget, owners) // jnp.take(total_weight, owners))
    in_zone = owners == zone_pick
    last_in_zone = in_zone & (host_rank == jnp.take(hosted, owners) - 1)
    lengths = jnp.where(last_in_zone, 1, lengths)
    needed = onehot * (lengths + 1)[:, None]
    cache_start = jnp.sum((jnp.cumsum(needed, axis=0) - needed) * onehot, axis=1)
    used = jnp.sum(needed, axis=0)
    cache_start = jnp.where(in_zone, cache_start + ROWS - jnp.take(used, owners), cache_start)
    return (owners.astype(jnp.int32), lengths.astype(jnp.int32), cache_start.astype(jnp.int32))


def draw_lengths(key, part):
    return layout_ints(key)[1]


def draw_owners(key, part):
    return layout_ints(key)[0]


def draw_cache_start(key, part):
    return layout_ints(key)[2]


def draw_project_in(key, part):
    base = jax.random.normal(jax.random.fold_in(key, 3), (3, D, D), jnp.float32)
    base = jnp.clip(base, -6.0, 6.0) * D ** (-0.5)
    return base.astype(jnp.bfloat16)


def draw_kv_cache(key, part):
    base = jax.random.normal(jax.random.fold_in(key, 5), (2, CACHE_ROWS, D), jnp.float32)
    base = jnp.clip(base, -6.0, 6.0)
    return base.astype(jnp.bfloat16)


def steps_of(key, shape, cuts, low, largest):
    loudness, own = 1.0, jax.random.fold_in(key, 6)
    for dim, shards_of in cuts:
        heights = jnp.exp(jax.random.uniform(jax.random.fold_in(own, dim), (shards_of,), jnp.float32, low / len(cuts), largest / len(cuts)))
        loudness = loudness * jnp.repeat(heights, shape[dim] // shards_of).reshape([-1 if axis == dim else 1 for axis in range(len(shape))])
    return loudness


def normal_values(key, dims, scale, reach, cuts=(), held_as=jnp.bfloat16):
    entries = jax.random.normal(key, dims, jnp.float32) * scale
    if len(cuts) > 0:
        entries = steps_of(key, dims, cuts, -0.22, 0.18) * entries
    return jnp.clip(entries, min=-reach, max=reach).astype(held_as)


def setup_inputs(seed: int = 0) -> dict:
    key_of = jax.random.split(jax.random.key(seed), 12)
    return {
        "tokens": normal_values(key_of[0], (REQUESTS, D), 1.0, 6.0, ((0, 32),)),
        "attn_gain": jnp.clip(1.0 + 0.18 * jax.random.normal(key_of[1], (D,), jnp.float32), 0.099609375, 1.8984375).astype(jnp.bfloat16),
        "mlp_gain": jnp.clip(1.0 + 0.18 * jax.random.normal(key_of[2], (D,), jnp.float32), 0.099609375, 1.8984375).astype(jnp.bfloat16),
        "project_in": draw_project_in(jax.random.fold_in(key_of[11], 71), 0),
        "project_out": normal_values(key_of[4], (D, D), D ** -0.5, 0.125, ((0, 8),)),
        "gate_up": normal_values(key_of[5], (2, D, FF), D ** -0.5, 0.125, ((2, 8),)),
        "project_down": normal_values(key_of[6], (FF, D), FF ** -0.5, 0.0625, ((0, 8),)),
        "kv_cache": draw_kv_cache(jax.random.fold_in(key_of[11], 71), 0),
        "lengths": draw_lengths(jax.random.fold_in(key_of[11], 71), 0),
        "owners": draw_owners(jax.random.fold_in(key_of[11], 71), 0),
        "cache_start": draw_cache_start(jax.random.fold_in(key_of[11], 71), 0),
    }


NORM_EPS = 1e-05
ROPE_BASE = 130000.0

def scaled_norm(values, scales):
    wide = values.astype(jnp.float32)
    factor = lax.rsqrt(lax.optimization_barrier(jnp.mean(wide * wide, axis=-1, keepdims=True)) + NORM_EPS)
    return (wide * factor * scales.astype(jnp.float32)).astype(jnp.bfloat16)

def rotate(values, positions, head_size):
    half_size = head_size // 2
    freqs = ROPE_BASE ** (-(jnp.arange(half_size, dtype=jnp.float32) * 2.0 / head_size))
    angles = positions.astype(jnp.float32)[:, None] * freqs[None, :]
    cosine = jnp.cos(angles)[:, None, :]
    sine = jnp.sin(angles)[:, None, :]
    first = values[..., :half_size]
    second = values[..., half_size:]
    return jnp.concatenate([first * cosine - second * sine, second * cosine + first * sine], axis=-1)

def reference(tokens, attn_gain, mlp_gain, project_in, project_out, gate_up, project_down, kv_cache, lengths, owners, cache_start):
    normed = scaled_norm(tokens, attn_gain)
    projected = jnp.einsum('rd,cde->rce', normed.astype(jnp.float32), project_in.astype(jnp.float32))
    request_count = tokens.shape[0]
    queries = rotate(projected[:, 0].reshape(request_count, HEADS, HD), lengths, HD).astype(jnp.bfloat16)
    keys_new = rotate(projected[:, 1].reshape(request_count, HEADS, HD), lengths, HD).astype(jnp.bfloat16)
    values_new = projected[:, 2].reshape(request_count, HEADS, HD).astype(jnp.bfloat16)
    padded = jnp.pad(kv_cache, ((0, 0), (0, MAXLEN), (0, 0)))
    starts = (owners * ROWS + cache_start).astype(jnp.int32)
    scale = 1.0 / HD ** 0.5

    def attend(item):
        query_row, key_row, value_row, start_row, length_row = item
        window = lax.dynamic_slice(padded, (jnp.int32(0), start_row.astype(jnp.int32), jnp.int32(0)), (2, MAXLEN, D))
        past_keys = window[0].astype(jnp.float32).reshape(MAXLEN, HEADS, HD)
        past_values = window[1].astype(jnp.float32).reshape(MAXLEN, HEADS, HD)
        query_wide = query_row.astype(jnp.float32)
        scores = jnp.einsum('he,phe->hp', query_wide, past_keys, precision=lax.Precision.HIGHEST) * scale
        live = (jnp.arange(MAXLEN) < length_row)[None, :]
        scores = jnp.where(live, scores, -jnp.inf)
        own = lax.optimization_barrier(jnp.sum(query_wide * key_row.astype(jnp.float32), axis=-1)) * scale
        top = jnp.maximum(lax.optimization_barrier(jnp.max(scores, axis=-1)), own)
        weights = jnp.where(live, jnp.exp(scores - top[:, None]), 0.0)
        own_weight = jnp.exp(own - top)
        total = lax.optimization_barrier(jnp.sum(weights, axis=-1)) + own_weight
        summed = jnp.einsum('hp,phe->he', weights, past_values, precision=lax.Precision.HIGHEST)
        summed = summed + own_weight[:, None] * value_row.astype(jnp.float32)
        attended = (summed / total[:, None]).astype(jnp.bfloat16).reshape(D)
        return (attended, top + jnp.log(total))
    attention, log_sum_exp = lax.map(attend, (queries, keys_new, values_new, starts, lengths))
    target_rows = (starts + lengths).astype(jnp.int32)
    kv_updated = kv_cache.at[0, target_rows].set(keys_new.reshape(request_count, D))
    kv_updated = kv_updated.at[1, target_rows].set(values_new.reshape(request_count, D))
    resid = (tokens.astype(jnp.float32) + jnp.dot(attention, project_out, preferred_element_type=jnp.float32)).astype(jnp.bfloat16)
    normed_mlp = scaled_norm(resid, mlp_gain)
    gate = jnp.dot(normed_mlp, gate_up[0], preferred_element_type=jnp.float32)
    upward = jnp.dot(normed_mlp, gate_up[1], preferred_element_type=jnp.float32)
    inner = (jax.nn.silu(gate) * upward).astype(jnp.bfloat16)
    hidden_states = (resid.astype(jnp.float32) + jnp.dot(inner, project_down, preferred_element_type=jnp.float32)).astype(jnp.bfloat16)
    return (hidden_states, log_sum_exp, kv_updated)
```

```python
import functools
import math

import jax
import jax.numpy as jnp
from jax import lax
from jax.experimental import pallas as pl
from jax.experimental.pallas import tpu as pltpu
from jax.sharding import PartitionSpec as P

HD = 64
NORM_EPS = 1e-05
ROPE_BASE = 130000.0
MASK_LOW = -1e30
BF = jnp.bfloat16
F32 = jnp.float32
LANES = 128
Q_TILE = 32
P_TILE = 512


def round_up(count, step):
    return (count + step - 1) // step * step


def dot(left, right):
    return jnp.dot(left, right, preferred_element_type=F32)


def dot_nt(left, right):
    return lax.dot_general(left, right, (((1,), (1,)), ((), ())), preferred_element_type=F32)


def dot_tn(left, right):
    return lax.dot_general(left, right, (((0,), (0,)), ((), ())), preferred_element_type=F32)


def one_hot(row_count, slots):
    rows = lax.broadcasted_iota(jnp.int32, (row_count, slots.shape[1]), 0)
    return jnp.where(rows == slots, 1.0, 0.0).astype(BF)


def swap(values, axis_name, offset):
    count = lax.axis_size(axis_name)
    return lax.ppermute(values, axis_name, [(i, i ^ offset) for i in range(count)])


def gather_tensor(block):
    count = lax.axis_size("tensor")
    pieces = [None] * count
    pieces[0] = block
    for k in range(2, count, 2):
        pieces[k] = swap(block, "tensor", k)
    for k in range(0, count, 2):
        pieces[k + 1] = swap(pieces[k], "tensor", 1)
    return pieces


def reduce_tensor(keep, send):
    count = lax.axis_size("tensor")
    came = swap(send, "tensor", 1)
    joined = [(keep[k].astype(F32) + came[k].astype(F32)).astype(BF) for k in range(count // 2)]
    return [joined[0]] + [swap(joined[k], "tensor", 2 * k) for k in range(1, count // 2)]


def relative(values, block_count, me):
    cut = values.reshape(block_count, -1)
    bit = 1
    while bit < block_count:
        split = cut.reshape(block_count // (2 * bit), 2, bit, -1)
        cut = jnp.where((me & bit) != 0, split[:, ::-1], split).reshape(block_count, -1)
        bit *= 2
    return cut.reshape(values.shape)


def scaled_norm(values, scales):
    wide = values.astype(F32)
    factor = lax.rsqrt(jnp.mean(wide * wide, axis=-1, keepdims=True) + NORM_EPS)
    return (wide * factor * scales.astype(F32)).astype(BF)


def qkv_kernel(piece_count, home_count, slot_rows, hop_count, *refs):
    pieces = refs[:piece_count]
    weights, cosine, sine, slots = refs[piece_count : piece_count + 4]
    home_ref = refs[piece_count + 4]
    out_refs = refs[piece_count + 5 :]
    normed = jnp.concatenate([piece[...] for piece in pieces], axis=0)
    width = weights.shape[2]
    lane = lax.broadcasted_iota(jnp.int32, (normed.shape[0], width), 1)
    low_half = (lane % HD) < HD // 2
    parts = []
    for c in range(3):
        projected = dot(normed, weights[c])
        if c < 2:
            ahead = pltpu.roll(projected, width - HD // 2, 1)
            behind = pltpu.roll(projected, HD // 2, 1)
            turned = jnp.where(low_half, -ahead, behind)
            projected = projected * cosine[...] + turned * sine[...]
        parts.append(projected.astype(BF))
    packed = jnp.concatenate(parts, axis=1)
    selector = one_hot(home_count + hop_count * slot_rows, slots[...])
    picked = dot(selector, packed).astype(BF)
    home_ref[...] = picked[:home_count]
    for k in range(hop_count):
        first = home_count + k * slot_rows
        out_refs[k][...] = picked[first : first + slot_rows]


def attend_tile(query, key, value, start, span, low, high, kv_ref, heads):
    rows, width = query.shape
    scale = 1.0 / math.sqrt(HD)
    lane_head = lax.broadcasted_iota(jnp.int32, (rows, width), 1) // HD
    masks = [lane_head == h for h in range(heads)]
    zero = jnp.zeros_like(query)
    stacked = jnp.concatenate([jnp.where(m, query, zero) for m in masks], axis=0)
    product = query.astype(F32) * key.astype(F32)
    own = jnp.concatenate(
        [jnp.sum(jnp.where(m, product, 0.0), axis=1, keepdims=True) for m in masks], axis=0
    ) * scale
    starts = jnp.concatenate([start] * heads, axis=0)
    spans = jnp.concatenate([span] * heads, axis=0)
    first_out = jnp.concatenate([value.astype(F32)] * heads, axis=0)

    def advance(step, carry):
        top, total, out = carry
        first = pl.multiple_of(step * P_TILE, P_TILE)
        keys = kv_ref[0, pl.ds(first, P_TILE), :]
        values = kv_ref[1, pl.ds(first, P_TILE), :]
        offset = lax.broadcasted_iota(jnp.int32, (1, P_TILE), 1) + first
        since = offset - starts
        live = (since >= 0) & (since < spans)
        scores = jnp.where(live, dot_nt(stacked, keys) * scale, MASK_LOW)
        new_top = jnp.maximum(top, jnp.max(scores, axis=1, keepdims=True))
        weights = jnp.exp(scores - new_top)
        factor = jnp.exp(top - new_top)
        total = total * factor + jnp.sum(weights, axis=1, keepdims=True)
        out = out * factor + dot(weights.astype(BF), values)
        return new_top, total, out

    top, total, out = lax.fori_loop(
        low, high, advance, (own, jnp.ones_like(own), first_out)
    )
    out = out / total
    log_sum = top + jnp.log(total)
    attended = jnp.zeros((rows, width), F32)
    lane = lax.broadcasted_iota(jnp.int32, (rows, LANES), 1)
    extra = jnp.zeros((rows, LANES), F32)
    for h in range(heads):
        attended = jnp.where(masks[h], out[h * rows : (h + 1) * rows], attended)
        rest = log_sum[h * rows : (h + 1) * rows]
        for part in range(3):
            piece = rest.astype(BF).astype(F32)
            rest = rest - piece
            extra = jnp.where(lane == part * heads + h, piece, extra)
    return jnp.concatenate([attended.astype(BF), extra.astype(BF)], axis=1)


def attend_all(bounds, packed, starts, spans, kv_ref, result, heads):
    width = heads * HD
    for tile in range(packed.shape[0] // Q_TILE):
        here = slice(tile * Q_TILE, (tile + 1) * Q_TILE)
        rows = packed[here]
        result[here, :] = attend_tile(
            rows[:, :width],
            rows[:, width : 2 * width],
            rows[:, 2 * width :],
            starts[here, :],
            spans[here, :],
            bounds[0, tile],
            bounds[1, tile],
            kv_ref,
            heads,
        )


def home_kernel(heads, bounds, packed, starts, spans, kv_ref, result):
    attend_all(bounds, packed[...], starts, spans, kv_ref, result, heads)


def far_kernel(heads, hop_count, sorted_count, bounds, *refs):
    arrived = jnp.concatenate([ref[...] for ref in refs[:hop_count]], axis=0)
    order, starts, spans, kv_ref = refs[hop_count : hop_count + 4]
    outs = refs[hop_count + 4 : 2 * hop_count + 4]
    scratch = refs[-1]
    mover = one_hot(sorted_count, order[...])
    in_order = dot(mover, arrived).astype(BF)
    attend_all(bounds, in_order, starts, spans, kv_ref, scratch, heads)
    back = dot_tn(mover, scratch[...]).astype(BF)
    slot_rows = arrived.shape[0] // hop_count
    for k in range(hop_count):
        outs[k][...] = back[k * slot_rows : (k + 1) * slot_rows]


def out_kernel(heads, hop_count, rows, slots, home, *refs):
    backs = refs[:hop_count]
    weights, keep_ref, send_ref, log_ref = refs[hop_count:]
    width = heads * HD
    both = jnp.concatenate([home[...]] + [ref[...] for ref in backs], axis=0)
    selector = one_hot(both.shape[0], slots[...])
    placed = dot_tn(selector, both)
    extra = placed[:, width:]
    log_sum = extra + pltpu.roll(extra, LANES - heads, 1) + pltpu.roll(extra, LANES - 2 * heads, 1)
    log_ref[...] = log_sum
    partial = dot(placed[:, :width].astype(BF), weights[...]).astype(BF)
    for k in range(partial.shape[0] // rows):
        ref = keep_ref if k % 2 == 0 else send_ref
        ref[k // 2] = partial[k * rows : (k + 1) * rows]


def mlp_kernel(piece_count, rows, *refs):
    pieces = refs[:piece_count]
    gate_up, down, keep_ref, send_ref, normed, total = refs[piece_count:]
    step = pl.program_id(0)

    @pl.when(step == 0)
    def _():
        for k, piece in enumerate(pieces):
            normed[k * rows : (k + 1) * rows, :] = piece[...]

    gate = dot(normed[...], gate_up[0])
    upward = dot(normed[...], gate_up[1])
    inner = (gate / (1.0 + jnp.exp(-gate)) * upward).astype(BF)
    partial = dot(inner, down[...])

    @pl.when(step == 0)
    def _():
        total[...] = partial

    @pl.when(step > 0)
    def _():
        total[...] += partial

    @pl.when(step == pl.num_programs(0) - 1)
    def _():
        for k in range(piece_count):
            ref = keep_ref if k % 2 == 0 else send_ref
            ref[k // 2] = total[k * rows : (k + 1) * rows, :].astype(BF)


def update_kernel(hop_count, width, home_rows, far_rows, home, *refs):
    far = refs[:hop_count]
    kv_in, kv_out = refs[hop_count:]
    block = kv_in.shape[1]
    position = lax.broadcasted_iota(jnp.int32, (block, 1), 0) + pl.program_id(0) * block
    fresh = jnp.concatenate([home[:, width:]] + [ref[:, width:] for ref in far], axis=0)
    targets = jnp.concatenate([home_rows[...], far_rows[...]], axis=1)
    hit = jnp.where(position == targets, 1.0, 0.0)
    written = jnp.max(hit, axis=1, keepdims=True) > 0.0
    values = dot(hit.astype(BF), fresh).astype(BF)
    kv_out[0] = jnp.where(written, values[:, :width], kv_in[0])
    kv_out[1] = jnp.where(written, values[:, width:], kv_in[1])


def tile_bounds(starts, spans, cache_rows):
    cut_start = starts.reshape(-1, Q_TILE)
    cut_end = jnp.where(spans > 0, starts + spans, 0).reshape(-1, Q_TILE)
    low = jnp.min(cut_start, axis=1) // P_TILE
    high = (jnp.max(cut_end, axis=1) + P_TILE - 1) // P_TILE
    return jnp.stack([jnp.minimum(low, high), high]).astype(jnp.int32)


def vmem(count):
    return [pl.BlockSpec(memory_space=pltpu.VMEM)] * count


def on_device(
    tokens,
    attn_gain,
    mlp_gain,
    project_in,
    project_out,
    gate_up,
    project_down,
    kv_cache,
    lengths,
    owners,
    cache_start,
):
    groups = lax.axis_size("dp")
    my_index = lax.axis_index("dp")
    tensor_count = lax.axis_size("tensor")
    me = lax.axis_index("tensor")
    rows, model_width = tokens.shape
    request_count = rows * tensor_count
    width = project_in.shape[2]
    heads = width // HD
    cache_rows = kv_cache.shape[1]
    home_count = round_up(request_count - request_count // 2, Q_TILE)
    hops = groups - 1
    capacity = (request_count // 2 + groups - 2) // (groups - 1)
    slot_rows = round_up(capacity, 16)
    far_count = hops * slot_rows
    sorted_count = round_up(min(hops * capacity, far_count), Q_TILE)
    params = functools.partial(pltpu.CompilerParams, vmem_limit_bytes=40 * 1024 * 1024)

    normed = scaled_norm(tokens, attn_gain)
    pieces = gather_tensor(normed)

    blocks = lambda values: values.reshape(groups, request_count)
    mine = lambda values: lax.dynamic_slice_in_dim(values, my_index * request_count, request_count)
    my_length, my_owner, my_start = (
        relative(mine(values), tensor_count, me) for values in (lengths, owners, cache_start)
    )
    before = (my_owner[:, None] == my_owner[None, :]) & (my_start[:, None] < my_start[None, :])
    rank = jnp.sum(before.astype(jnp.int32), axis=0)
    hop = my_owner ^ my_index
    slot = jnp.where(hop == 0, rank, home_count + (hop - 1) * slot_rows + rank)
    home_hit = slot[None, :] == jnp.arange(home_count)[:, None]
    pick = lambda hit, values: jnp.sum(jnp.where(hit, values, 0), axis=1)
    home_span = pick(home_hit, my_length[None, :])
    home_live = home_span > 0
    home_start = jnp.where(home_live, pick(home_hit, my_start[None, :]), cache_rows)

    all_here = blocks(owners) == my_index
    start_blocks, length_blocks = blocks(cache_start), blocks(lengths)
    ahead = all_here[:, :, None] & (start_blocks[:, :, None] < start_blocks[:, None, :])
    in_rank = jnp.sum(ahead.astype(jnp.int32), axis=1)
    in_hop = jnp.arange(groups)[:, None] ^ my_index
    in_slot = jnp.where(all_here & (in_hop != 0), (in_hop - 1) * slot_rows + in_rank, -1).reshape(-1)
    far_hit = in_slot[None, :] == jnp.arange(far_count)[:, None]
    far_span = pick(far_hit, lengths[None, :])
    far_start = jnp.where(far_span > 0, pick(far_hit, cache_start[None, :]), cache_rows)
    far_live = far_span > 0
    far_before = far_live[:, None] & (far_start[:, None] < far_start[None, :])
    far_order = jnp.where(far_live, jnp.sum(far_before.astype(jnp.int32), axis=0), -1)
    sort_hit = far_order[None, :] == jnp.arange(sorted_count)[:, None]
    sort_span = pick(sort_hit, far_span[None, :])
    sort_start = jnp.where(sort_span > 0, pick(sort_hit, far_start[None, :]), cache_rows)
    home_bounds = tile_bounds(home_start, home_span, cache_rows)
    far_bounds = tile_bounds(sort_start, sort_span, cache_rows)
    home_write = jnp.where(home_live, home_start + home_span, -1)[None, :]
    far_write = jnp.where(far_live, far_start + far_span, -1)[None, :]

    half = HD // 2
    freqs = ROPE_BASE ** (-(jnp.arange(half, dtype=F32) * 2.0 / HD))
    angles = my_length.astype(F32)[:, None] * freqs[None, :]
    cosine = jnp.tile(jnp.cos(angles), (1, width // half))
    sine = jnp.tile(jnp.sin(angles), (1, width // half))

    slots = slot[None, :]
    shape = jax.ShapeDtypeStruct
    packed_outs = pl.pallas_call(
        functools.partial(qkv_kernel, tensor_count, home_count, slot_rows, hops),
        out_shape=[shape((home_count, 3 * width), BF)] + [shape((slot_rows, 3 * width), BF)] * hops,
        in_specs=vmem(tensor_count + 4),
        out_specs=vmem(1 + hops),
        compiler_params=params(),
        name="qkv",
    )(*pieces, project_in, cosine, sine, slots)
    home_packed = packed_outs[0]
    arrived = [swap(packed_outs[k], "dp", k) for k in range(1, groups)]

    out_width = width + LANES
    smem = pl.BlockSpec(memory_space=pltpu.SMEM)
    home_att = pl.pallas_call(
        functools.partial(home_kernel, heads),
        out_shape=shape((home_count, out_width), BF),
        in_specs=[smem] + vmem(4),
        out_specs=vmem(1)[0],
        compiler_params=params(),
        cost_estimate=pl.CostEstimate(flops=2 * 10**9, bytes_accessed=4 * 2**20, transcendentals=10**6),
        name="home_attention",
    )(home_bounds, home_packed, home_start[:, None], home_span[:, None], kv_cache)
    far_outs = pl.pallas_call(
        functools.partial(far_kernel, heads, hops, sorted_count),
        out_shape=[shape((slot_rows, out_width), BF)] * hops,
        in_specs=[smem] + vmem(hops + 4),
        out_specs=vmem(hops),
        scratch_shapes=[pltpu.VMEM((sorted_count, out_width), BF)],
        compiler_params=params(),
        name="far_attention",
    )(far_bounds, *arrived, far_order[None, :], sort_start[:, None], sort_span[:, None], kv_cache)
    backs = [swap(far_outs[k - 1], "dp", k) for k in range(1, groups)]

    block = 512
    kv_spec = pl.BlockSpec((2, block, width), lambda i: (0, i, 0))
    fixed = lambda array: pl.BlockSpec(array.shape, lambda i: (0,) * array.ndim)
    kv_updated = pl.pallas_call(
        functools.partial(update_kernel, hops, width),
        grid=(cache_rows // block,),
        out_shape=shape(kv_cache.shape, BF),
        in_specs=[fixed(home_write), fixed(far_write), fixed(home_packed)]
        + [fixed(a) for a in arrived]
        + [kv_spec],
        out_specs=kv_spec,
        compiler_params=params(),
        cost_estimate=pl.CostEstimate(flops=2 * 10**9, bytes_accessed=8 * 2**20, transcendentals=0),
        name="cache_update",
    )(home_write, far_write, home_packed, *arrived, kv_cache)

    half_count = tensor_count // 2
    keep, send, log_rel = pl.pallas_call(
        functools.partial(out_kernel, heads, hops, rows),
        out_shape=[shape((half_count, rows, model_width), BF)] * 2
        + [shape((request_count, LANES), F32)],
        in_specs=vmem(3 + hops),
        out_specs=vmem(3),
        compiler_params=params(),
        name="project_out",
    )(slots, home_att, *backs, project_out)
    log_sum_exp = relative(log_rel.reshape(-1), tensor_count, me).reshape(log_rel.shape)[:, :heads]

    sums = reduce_tensor(keep, send)
    attn_mine = sum(piece.astype(F32) for piece in sums)
    resid = (tokens.astype(F32) + attn_mine).astype(BF)
    mlp_pieces = gather_tensor(scaled_norm(resid, mlp_gain))

    hidden = gate_up.shape[2]
    f_block = min(256, hidden)
    keep, send = pl.pallas_call(
        functools.partial(mlp_kernel, tensor_count, rows),
        grid=(hidden // f_block,),
        out_shape=[shape((half_count, rows, model_width), BF)] * 2,
        in_specs=[fixed(normed)] * tensor_count
        + [
            pl.BlockSpec((2, model_width, f_block), lambda i: (0, 0, i)),
            pl.BlockSpec((f_block, model_width), lambda i: (i, 0)),
        ],
        out_specs=[pl.BlockSpec((half_count, rows, model_width), lambda i: (0, 0, 0))] * 2,
        scratch_shapes=[
            pltpu.VMEM((request_count, model_width), BF),
            pltpu.VMEM((request_count, model_width), F32),
        ],
        compiler_params=params(),
        name="mlp",
    )(*mlp_pieces, gate_up, project_down)
    down_mine = sum(piece.astype(F32) for piece in reduce_tensor(keep, send))
    hidden_states = (resid.astype(F32) + down_mine).astype(BF)
    return (hidden_states, log_sum_exp, kv_updated)


def solution(mesh):
    placed = (
        P(("dp", "tensor"), None),
        P(),
        P(),
        P(None, None, "tensor"),
        P("tensor", None),
        P(None, None, "tensor"),
        P("tensor", None),
        P(None, "dp", "tensor"),
        P(),
        P(),
        P(),
    )
    return jax.shard_map(
        on_device,
        mesh=mesh,
        in_specs=placed,
        out_specs=(P(("dp", "tensor"), None), P("dp", "tensor"), P(None, "dp", "tensor")),
        check_vma=False,
    )
```

```python
import functools
import math

import jax
import jax.numpy as jnp
from jax import lax
from jax.experimental import pallas as pl
from jax.experimental.pallas import tpu as pltpu
from jax.sharding import PartitionSpec as P

HD = 64
NORM_EPS = 1e-05
ROPE_BASE = 130000.0
MASK_LOW = -1e30
BF = jnp.bfloat16
F32 = jnp.float32
LANES = 128
Q_TILE = 32
P_TILE = 512


def round_up(count, step):
    return (count + step - 1) // step * step


def dot(left, right):
    return jnp.dot(left, right, preferred_element_type=F32)


def dot_nt(left, right):
    return lax.dot_general(left, right, (((1,), (1,)), ((), ())), preferred_element_type=F32)


def dot_tn(left, right):
    return lax.dot_general(left, right, (((0,), (0,)), ((), ())), preferred_element_type=F32)


def one_hot(row_count, slots):
    rows = lax.broadcasted_iota(jnp.int32, (row_count, slots.shape[1]), 0)
    return jnp.where(rows == slots, 1.0, 0.0).astype(BF)


def swap(values, axis_name, offset):
    count = lax.axis_size(axis_name)
    return lax.ppermute(values, axis_name, [(i, i ^ offset) for i in range(count)])


def gather_tensor(block, beside=None):
    count = lax.axis_size("tensor")
    pieces = [None] * count
    pieces[0] = block
    for k in range(2, count, 2):
        pieces[k] = swap(block, "tensor", k)
    if beside is not None:
        pieces[::2], done = lax.optimization_barrier((pieces[::2], beside()))
    for k in range(0, count, 2):
        pieces[k + 1] = swap(pieces[k], "tensor", 1)
    return pieces if beside is None else (pieces, done)


def reduce_tensor(keep, send):
    count = lax.axis_size("tensor")
    came = swap(send, "tensor", 1)
    joined = [(keep[k].astype(F32) + came[k].astype(F32)).astype(BF) for k in range(count // 2)]
    return [joined[0]] + [swap(joined[k], "tensor", 2 * k) for k in range(1, count // 2)]


def norm_kernel(tokens, gain, result):
    wide = tokens[...].astype(F32)
    factor = lax.rsqrt(jnp.mean(wide * wide, axis=-1, keepdims=True) + NORM_EPS)
    result[...] = (wide * factor * gain[...].astype(F32)).astype(BF)


def column_of(row):
    count = row.shape[1]
    shape = (count, count)
    same = lax.broadcasted_iota(jnp.int32, shape, 0) == lax.broadcasted_iota(jnp.int32, shape, 1)
    return jnp.sum(jnp.where(same, row, 0.0), axis=1, keepdims=True)


def row_of(column):
    count = column.shape[0]
    shape = (count, count)
    same = lax.broadcasted_iota(jnp.int32, shape, 0) == lax.broadcasted_iota(jnp.int32, shape, 1)
    return jnp.sum(jnp.where(same, column, 0.0), axis=0, keepdims=True)


def picked(row_count, ranks, values):
    rows = lax.broadcasted_iota(jnp.int32, (row_count, ranks.shape[1]), 0).astype(F32)
    return [
        jnp.sum(jnp.where(rows == ranks, value, 0.0), axis=1, keepdims=True) for value in values
    ]


def plan_kernel(sizes, lengths, owners, starts, freqs, *outs):
    groups, count, home_count, slot_rows, sorted_count, cache_rows = sizes
    (
        slots_ref,
        cos_ref,
        sin_ref,
        home_start,
        home_span,
        home_write,
        home_bounds,
        far_order,
        sort_start,
        sort_span,
        far_write,
        far_bounds,
    ) = outs
    here = lax.axis_index("dp")

    def block(ref, index):
        return ref[:, pl.ds(pl.multiple_of(index * count, LANES), count)]

    def ranks_of(owner, start):
        owner_column, start_column = column_of(owner), column_of(start)
        before = (owner_column == owner) & (start_column < start)
        return jnp.sum(jnp.where(before, 1.0, 0.0), axis=0, keepdims=True)

    def put_ranges(start_ref, span_ref, bounds_ref, start, span):
        start_ref[...] = start.astype(jnp.int32)
        span_ref[...] = span.astype(jnp.int32)
        for tile in range(start.shape[0] // Q_TILE):
            cut = slice(tile * Q_TILE, (tile + 1) * Q_TILE)
            live = span[cut] > 0.0
            low = jnp.min(start[cut]).astype(jnp.int32) // P_TILE
            last = jnp.max(jnp.where(live, start[cut] + span[cut], 0.0)).astype(jnp.int32)
            high = (last + (P_TILE - 1)) // P_TILE
            bounds_ref[0, tile] = jnp.minimum(low, high)
            bounds_ref[1, tile] = high

    my_owner = block(owners, here)
    my_start = block(starts, here).astype(F32)
    my_length = block(lengths, here).astype(F32)
    rank = ranks_of(my_owner.astype(F32), my_start)
    hop = my_owner ^ here
    slot = jnp.where(hop == 0, rank, (hop - 1).astype(F32) * slot_rows + (rank + home_count))
    slots_ref[...] = slot.astype(jnp.int32)
    angles = column_of(my_length) * freqs[...]
    cos_ref[...] = jnp.cos(angles)
    sin_ref[...] = jnp.sin(angles)
    start, span = picked(home_count, slot, [my_start, my_length])
    live = span > 0.0
    start = jnp.where(live, start, float(cache_rows))
    put_ranges(home_start, home_span, home_bounds, start, span)
    home_write[...] = row_of(jnp.where(live, start + span, -1.0)).astype(jnp.int32)

    far = []
    for k in range(1, groups):
        source = here ^ k
        owner = block(owners, source)
        start = block(starts, source).astype(F32)
        rank = ranks_of(owner.astype(F32), start)
        rank = jnp.where(owner == here, rank, -1.0)
        far.append(picked(slot_rows, rank, [start, block(lengths, source).astype(F32)]))
    start = jnp.concatenate([pair[0] for pair in far], axis=0)
    span = jnp.concatenate([pair[1] for pair in far], axis=0)
    live = span > 0.0
    start = jnp.where(live, start, float(cache_rows))
    far_write[...] = row_of(jnp.where(live, start + span, -1.0)).astype(jnp.int32)
    start_row, span_row = row_of(start), row_of(span)
    order = jnp.sum(jnp.where(start < start_row, 1.0, 0.0), axis=0, keepdims=True)
    order = jnp.where(span_row > 0.0, order, -1.0)
    far_order[...] = order.astype(jnp.int32)
    start, span = picked(sorted_count, order, [start_row, span_row])
    start = jnp.where(span > 0.0, start, float(cache_rows))
    put_ranges(sort_start, sort_span, far_bounds, start, span)


def qkv_kernel(piece_count, home_count, slot_rows, hop_count, *refs):
    pieces = refs[:piece_count]
    weights, cosine, sine, slots = refs[piece_count : piece_count + 4]
    home_ref = refs[piece_count + 4]
    out_refs = refs[piece_count + 5 : -1]
    normed = refs[-1]
    me = lax.axis_index("tensor")
    rows = pieces[0].shape[0]
    for k, piece in enumerate(pieces):
        normed[pl.ds(pl.multiple_of((me ^ k) * rows, rows), rows), :] = piece[...]
    width = weights.shape[2]
    lane = lax.broadcasted_iota(jnp.int32, (normed.shape[0], width), 1)
    low_half = (lane % HD) < HD // 2
    wide = lambda ref: jnp.concatenate([ref[...]] * (width // LANES), axis=1)
    parts = []
    for c in range(3):
        projected = dot(normed[...], weights[c])
        if c < 2:
            ahead = pltpu.roll(projected, width - HD // 2, 1)
            behind = pltpu.roll(projected, HD // 2, 1)
            turned = jnp.where(low_half, -ahead, behind)
            projected = projected * wide(cosine) + turned * wide(sine)
        parts.append(projected.astype(BF))
    packed = jnp.concatenate(parts, axis=1)
    selector = one_hot(home_count + hop_count * slot_rows, slots[...])
    chosen = dot(selector, packed).astype(BF)
    home_ref[...] = chosen[:home_count]
    for k in range(hop_count):
        first = home_count + k * slot_rows
        out_refs[k][...] = chosen[first : first + slot_rows]


def attend_tile(query, key, value, start, span, low, high, kv_ref, heads):
    rows, width = query.shape
    scale = 1.0 / math.sqrt(HD)
    lane_head = lax.broadcasted_iota(jnp.int32, (rows, width), 1) // HD
    masks = [lane_head == h for h in range(heads)]
    zero = jnp.zeros_like(query)
    stacked = jnp.concatenate([jnp.where(m, query, zero) for m in masks], axis=0)
    product = query.astype(F32) * key.astype(F32)
    own = jnp.concatenate(
        [jnp.sum(jnp.where(m, product, 0.0), axis=1, keepdims=True) for m in masks], axis=0
    ) * scale
    starts = jnp.concatenate([start] * heads, axis=0)
    spans = jnp.concatenate([span] * heads, axis=0)
    first_out = jnp.concatenate([value.astype(F32)] * heads, axis=0)

    def advance(step, carry):
        top, total, out = carry
        first = pl.multiple_of(step * P_TILE, P_TILE)
        keys = kv_ref[0, pl.ds(first, P_TILE), :]
        values = kv_ref[1, pl.ds(first, P_TILE), :]
        offset = lax.broadcasted_iota(jnp.int32, (1, P_TILE), 1) + first
        since = offset - starts
        live = (since >= 0) & (since < spans)
        scores = jnp.where(live, dot_nt(stacked, keys) * scale, MASK_LOW)
        new_top = jnp.maximum(top, jnp.max(scores, axis=1, keepdims=True))
        weights = jnp.exp(scores - new_top)
        factor = jnp.exp(top - new_top)
        total = total * factor + jnp.sum(weights, axis=1, keepdims=True)
        out = out * factor + dot(weights.astype(BF), values)
        return new_top, total, out

    top, total, out = lax.fori_loop(
        low, high, advance, (own, jnp.ones_like(own), first_out)
    )
    out = out / total
    log_sum = top + jnp.log(total)
    attended = jnp.zeros((rows, width), F32)
    lane = lax.broadcasted_iota(jnp.int32, (rows, LANES), 1)
    extra = jnp.zeros((rows, LANES), F32)
    for h in range(heads):
        attended = jnp.where(masks[h], out[h * rows : (h + 1) * rows], attended)
        rest = log_sum[h * rows : (h + 1) * rows]
        for part in range(3):
            piece = rest.astype(BF).astype(F32)
            rest = rest - piece
            extra = jnp.where(lane == part * heads + h, piece, extra)
    return jnp.concatenate([attended.astype(BF), extra.astype(BF)], axis=1)


def attend_all(bounds, packed, starts, spans, kv_ref, result, heads):
    width = heads * HD
    for tile in range(packed.shape[0] // Q_TILE):
        here = slice(tile * Q_TILE, (tile + 1) * Q_TILE)
        rows = packed[here]
        result[here, :] = attend_tile(
            rows[:, :width],
            rows[:, width : 2 * width],
            rows[:, 2 * width :],
            starts[here, :],
            spans[here, :],
            bounds[0, tile],
            bounds[1, tile],
            kv_ref,
            heads,
        )


def home_kernel(heads, bounds, packed, starts, spans, kv_ref, result):
    attend_all(bounds, packed[...], starts, spans, kv_ref, result, heads)


def far_kernel(heads, hop_count, sorted_count, bounds, *refs):
    arrived = jnp.concatenate([ref[...] for ref in refs[:hop_count]], axis=0)
    order, starts, spans, kv_ref, _ = refs[hop_count : hop_count + 5]
    outs = refs[hop_count + 5 : 2 * hop_count + 5]
    scratch = refs[-1]
    mover = one_hot(sorted_count, order[...])
    in_order = dot(mover, arrived).astype(BF)
    attend_all(bounds, in_order, starts, spans, kv_ref, scratch, heads)
    back = dot_tn(mover, scratch[...]).astype(BF)
    slot_rows = arrived.shape[0] // hop_count
    for k in range(hop_count):
        outs[k][...] = back[k * slot_rows : (k + 1) * slot_rows]


def put_chunks(keep_ref, send_ref, partial, rows):
    me = lax.axis_index("tensor")
    for k in range(partial.shape[0] // rows):
        ref = keep_ref if k % 2 == 0 else send_ref
        ref[k // 2] = partial[pl.ds(pl.multiple_of((me ^ k) * rows, rows), rows), :]


def out_first_kernel(heads, hop_count, rows, slots, home, *refs):
    backs = refs[:hop_count]
    weights, keep_ref, send_ref, placed_ref, log_ref, partial = refs[hop_count:]
    width = heads * HD
    half = keep_ref.shape[2]
    both = jnp.concatenate([home[...]] + [ref[...] for ref in backs], axis=0)
    placed = dot_tn(one_hot(both.shape[0], slots[...]), both)
    extra = placed[:, width:]
    log_ref[...] = (
        extra + pltpu.roll(extra, LANES - heads, 1) + pltpu.roll(extra, LANES - 2 * heads, 1)
    )
    attention = placed[:, :width].astype(BF)
    placed_ref[...] = attention
    partial[...] = dot(attention, weights[:, :half]).astype(BF)
    put_chunks(keep_ref, send_ref, partial, rows)


def out_second_kernel(rows, attention, weights, keep_ref, send_ref, partial):
    half = keep_ref.shape[2]
    partial[...] = dot(attention[...], weights[:, half:]).astype(BF)
    put_chunks(keep_ref, send_ref, partial, rows)


def scaled_rows(pieces, gain):
    wide = jnp.concatenate([piece[...] for piece in pieces], axis=0).astype(F32)
    return (wide * gain[...].astype(F32)).astype(BF), jnp.sum(wide * wide, axis=1, keepdims=True)


def gate_kernel(piece_count, *refs):
    pieces = refs[:piece_count]
    gain, gate_up, gate_ref, up_ref, square_ref = refs[piece_count:]
    half = pieces[0].shape[1]
    scaled, square_ref[...] = scaled_rows(pieces, gain)
    gate_ref[...] = dot(scaled, gate_up[0, :half])
    up_ref[...] = dot(scaled, gate_up[1, :half])


def down_first_kernel(piece_count, rows, *refs):
    pieces = refs[:piece_count]
    gain, gate_up, gate_ref, up_ref, square_ref, down = refs[piece_count : piece_count + 6]
    inner_ref, keep_ref, send_ref = refs[piece_count + 6 :]
    half = pieces[0].shape[1]
    scaled, squares = scaled_rows(pieces, gain)
    factor = lax.rsqrt((squares + square_ref[...]) / (2 * half) + NORM_EPS)
    gate = (gate_ref[...] + dot(scaled, gate_up[0, half:])) * factor
    upward = (up_ref[...] + dot(scaled, gate_up[1, half:])) * factor
    inner = (gate / (1.0 + jnp.exp(-gate)) * upward).astype(BF)
    inner_ref[...] = inner
    partial = dot(inner, down[:, :half]).astype(BF)
    put_relative(keep_ref, send_ref, partial, rows)


def down_second_kernel(rows, inner, down, keep_ref, send_ref):
    half = keep_ref.shape[2]
    partial = dot(inner[...], down[:, half:]).astype(BF)
    put_relative(keep_ref, send_ref, partial, rows)


def put_relative(keep_ref, send_ref, partial, rows):
    for k in range(partial.shape[0] // rows):
        ref = keep_ref if k % 2 == 0 else send_ref
        ref[k // 2] = partial[k * rows : (k + 1) * rows]


def update_kernel(hop_count, width, home_rows, far_rows, home, *refs):
    far = refs[:hop_count]
    kv_in, kv_out = refs[hop_count:]
    block = kv_in.shape[1]
    position = lax.broadcasted_iota(jnp.int32, (block, 1), 0) + pl.program_id(0) * block
    fresh = jnp.concatenate([home[:, width:]] + [ref[:, width:] for ref in far], axis=0)
    targets = jnp.concatenate([home_rows[...], far_rows[...]], axis=1)
    hit = jnp.where(position == targets, 1.0, 0.0)
    written = jnp.max(hit, axis=1, keepdims=True) > 0.0
    values = dot(hit.astype(BF), fresh).astype(BF)
    kv_out[0] = jnp.where(written, values[:, :width], kv_in[0])
    kv_out[1] = jnp.where(written, values[:, width:], kv_in[1])


def vmem(count):
    return [pl.BlockSpec(memory_space=pltpu.VMEM)] * count


def on_device(
    tokens,
    attn_gain,
    mlp_gain,
    project_in,
    project_out,
    gate_up,
    project_down,
    kv_cache,
    lengths,
    owners,
    cache_start,
):
    groups = lax.axis_size("dp")
    my_index = lax.axis_index("dp")
    tensor_count = lax.axis_size("tensor")
    me = lax.axis_index("tensor")
    rows, model_width = tokens.shape
    request_count = rows * tensor_count
    width = project_in.shape[2]
    heads = width // HD
    cache_rows = kv_cache.shape[1]
    home_count = round_up(request_count - request_count // 2, Q_TILE)
    hops = groups - 1
    capacity = (request_count // 2 + groups - 2) // (groups - 1)
    slot_rows = round_up(capacity, 16)
    far_count = hops * slot_rows
    sorted_count = round_up(min(hops * capacity, far_count), Q_TILE)
    shape = jax.ShapeDtypeStruct
    smem = pl.BlockSpec(memory_space=pltpu.SMEM)
    anywhere = pl.BlockSpec(memory_space=pl.ANY)

    def params(mebibytes):
        return pltpu.CompilerParams(vmem_limit_bytes=mebibytes * 1024 * 1024)

    def cost(flops, bytes_accessed, transcendentals=0):
        return pl.CostEstimate(
            flops=flops, bytes_accessed=bytes_accessed, transcendentals=transcendentals
        )

    normed = pl.pallas_call(
        norm_kernel,
        out_shape=shape(tokens.shape, BF),
        in_specs=vmem(2),
        out_specs=vmem(1)[0],
        compiler_params=params(16),
        name="attn_norm",
    )(tokens, attn_gain[None, :])

    ints = lambda *dims: shape(dims, jnp.int32)
    freqs = ROPE_BASE ** (-((jnp.arange(LANES) % (HD // 2)).astype(F32) * 2.0 / HD))
    plan = lambda: pl.pallas_call(
        functools.partial(
            plan_kernel,
            (groups, request_count, home_count, slot_rows, sorted_count, cache_rows),
        ),
        out_shape=[
            ints(1, request_count),
            shape((request_count, LANES), F32),
            shape((request_count, LANES), F32),
            ints(home_count, 1),
            ints(home_count, 1),
            ints(1, home_count),
            ints(2, home_count // Q_TILE),
            ints(1, far_count),
            ints(sorted_count, 1),
            ints(sorted_count, 1),
            ints(1, far_count),
            ints(2, sorted_count // Q_TILE),
        ],
        in_specs=vmem(4),
        out_specs=vmem(6) + [smem] + vmem(4) + [smem],
        compiler_params=params(16),
        cost_estimate=cost(4 * 10**9, 10**6, 10**5),
        name="plan",
    )(lengths[None, :], owners[None, :], cache_start[None, :], freqs[None, :])
    pieces, planned = gather_tensor(normed, plan)
    (
        slots,
        cosine,
        sine,
        home_start,
        home_span,
        home_write,
        home_bounds,
        far_order,
        sort_start,
        sort_span,
        far_write,
        far_bounds,
    ) = planned

    packed_outs = pl.pallas_call(
        functools.partial(qkv_kernel, tensor_count, home_count, slot_rows, hops),
        out_shape=[shape((home_count, 3 * width), BF)] + [shape((slot_rows, 3 * width), BF)] * hops,
        in_specs=vmem(tensor_count + 4),
        out_specs=vmem(1 + hops),
        scratch_shapes=[pltpu.VMEM((request_count, model_width), BF)],
        compiler_params=params(24),
        name="qkv",
    )(*pieces, project_in, cosine, sine, slots)
    home_packed = packed_outs[0]
    arrived = [swap(packed_outs[k], "dp", k) for k in range(1, groups)]

    out_width = width + LANES
    home_att = pl.pallas_call(
        functools.partial(home_kernel, heads),
        out_shape=shape((home_count, out_width), BF),
        in_specs=[smem] + vmem(4),
        out_specs=vmem(1)[0],
        compiler_params=params(16),
        cost_estimate=cost(2 * 10**9, 4 * 2**20, 10**6),
        name="home_attention",
    )(home_bounds, home_packed, home_start, home_span, kv_cache)
    far_outs = pl.pallas_call(
        functools.partial(far_kernel, heads, hops, sorted_count),
        out_shape=[shape((slot_rows, out_width), BF)] * hops,
        in_specs=[smem] + vmem(hops + 4) + [anywhere],
        out_specs=vmem(hops),
        scratch_shapes=[pltpu.VMEM((sorted_count, out_width), BF)],
        compiler_params=params(16),
        name="far_attention",
    )(far_bounds, *arrived, far_order, sort_start, sort_span, kv_cache, home_att)
    backs = [swap(far_outs[k - 1], "dp", k) for k in range(1, groups)]

    block = 512
    kv_spec = pl.BlockSpec((2, block, width), lambda i: (0, i, 0))
    fixed = lambda array: pl.BlockSpec(array.shape, lambda i: (0,) * array.ndim)
    kv_updated = pl.pallas_call(
        functools.partial(update_kernel, hops, width),
        grid=(cache_rows // block,),
        out_shape=shape(kv_cache.shape, BF),
        in_specs=[fixed(home_write), fixed(far_write), fixed(home_packed)]
        + [fixed(a) for a in arrived]
        + [kv_spec],
        out_specs=kv_spec,
        compiler_params=params(16),
        cost_estimate=cost(2 * 10**9, 8 * 2**20),
        name="cache_update",
    )(home_write, far_write, home_packed, *arrived, kv_cache)
    home_att, kv_updated = lax.optimization_barrier((home_att, kv_updated))

    half_count = tensor_count // 2
    half = model_width // 2
    halves = [shape((half_count, rows, half), BF)] * 2
    partial_scratch = [pltpu.VMEM((request_count, half), BF)]
    keep, send, attention, log_sum = pl.pallas_call(
        functools.partial(out_first_kernel, heads, hops, rows),
        out_shape=halves + [shape((request_count, width), BF), shape((request_count, LANES), F32)],
        in_specs=vmem(3 + hops),
        out_specs=vmem(4),
        scratch_shapes=partial_scratch,
        compiler_params=params(16),
        name="project_out_first",
    )(slots, home_att, *backs, project_out)
    log_sum_exp = log_sum[:, :heads]
    sums_first = reduce_tensor(keep, send)
    keep, send = pl.pallas_call(
        functools.partial(out_second_kernel, rows),
        out_shape=halves,
        in_specs=vmem(2),
        out_specs=vmem(2),
        scratch_shapes=partial_scratch,
        compiler_params=params(16),
        name="project_out_second",
    )(attention, project_out)
    sums_second = reduce_tensor(keep, send)

    def add_up(base, sums):
        return (base.astype(F32) + sum(piece.astype(F32) for piece in sums)).astype(BF)

    resid_first = add_up(tokens[:, :half], sums_first)
    resid_second = add_up(tokens[:, half:], sums_second)
    pieces_first = gather_tensor(resid_first)
    pieces_second = gather_tensor(resid_second)
    hidden = gate_up.shape[2]
    gate_part, up_part, squares = pl.pallas_call(
        functools.partial(gate_kernel, tensor_count),
        out_shape=[shape((request_count, hidden), F32)] * 2 + [shape((request_count, 1), F32)],
        in_specs=vmem(tensor_count + 2),
        out_specs=vmem(3),
        compiler_params=params(24),
        cost_estimate=cost(2 * 10**9, 4 * 2**20),
        name="gate_up_first",
    )(*pieces_first, mlp_gain[None, :half], gate_up)
    inner, keep, send = pl.pallas_call(
        functools.partial(down_first_kernel, tensor_count, rows),
        out_shape=[shape((request_count, hidden), BF)] + halves,
        in_specs=vmem(tensor_count + 6),
        out_specs=vmem(3),
        compiler_params=params(32),
        name="down_first",
    )(*pieces_second, mlp_gain[None, half:], gate_up, gate_part, up_part, squares, project_down)
    sums_first = reduce_tensor(keep, send)
    keep, send = pl.pallas_call(
        functools.partial(down_second_kernel, rows),
        out_shape=halves,
        in_specs=vmem(2),
        out_specs=vmem(2),
        compiler_params=params(16),
        name="down_second",
    )(inner, project_down)
    sums_second = reduce_tensor(keep, send)
    hidden_states = jnp.concatenate(
        [add_up(resid_first, sums_first), add_up(resid_second, sums_second)], axis=1
    )
    return (hidden_states, log_sum_exp, kv_updated)


def solution(mesh):
    placed = (
        P(("dp", "tensor"), None),
        P(),
        P(),
        P(None, None, "tensor"),
        P("tensor", None),
        P(None, None, "tensor"),
        P("tensor", None),
        P(None, "dp", "tensor"),
        P(),
        P(),
        P(),
    )
    return jax.shard_map(
        on_device,
        mesh=mesh,
        in_specs=placed,
        out_specs=(P(("dp", "tensor"), None), P("dp", "tensor"), P(None, "dp", "tensor")),
        check_vma=False,
    )
```

```python
import functools
import math

import jax
import jax.numpy as jnp
from jax import lax
from jax.experimental import pallas as pl
from jax.experimental.pallas import tpu as pltpu
from jax.sharding import PartitionSpec as P

HD = 64
NORM_EPS = 1e-05
ROPE_BASE = 130000.0
MASK_LOW = -1e30
BF = jnp.bfloat16
F32 = jnp.float32
LANES = 128
Q_TILE = 32
P_TILE = 512


def round_up(count, step):
    return (count + step - 1) // step * step


def dot(left, right):
    return jnp.dot(left, right, preferred_element_type=F32)


def dot_nt(left, right):
    return lax.dot_general(left, right, (((1,), (1,)), ((), ())), preferred_element_type=F32)


def dot_tn(left, right):
    return lax.dot_general(left, right, (((0,), (0,)), ((), ())), preferred_element_type=F32)


def one_hot(row_count, slots):
    rows = lax.broadcasted_iota(jnp.int32, (row_count, slots.shape[1]), 0)
    return jnp.where(rows == slots, 1.0, 0.0).astype(BF)


def swap(values, axis_name, offset):
    count = lax.axis_size(axis_name)
    return lax.ppermute(values, axis_name, [(i, i ^ offset) for i in range(count)])


def gather_tensor(block, beside=None):
    count = lax.axis_size("tensor")
    pieces = [None] * count
    pieces[0] = block
    for k in range(2, count, 2):
        pieces[k] = swap(block, "tensor", k)
    if beside is not None:
        pieces[::2], done = lax.optimization_barrier((pieces[::2], beside()))
    for k in range(0, count, 2):
        pieces[k + 1] = swap(pieces[k], "tensor", 1)
    return pieces if beside is None else (pieces, done)


def reduce_tensor(keep, send):
    count = lax.axis_size("tensor")
    came = swap(send, "tensor", 1)
    joined = [(keep[k].astype(F32) + came[k].astype(F32)).astype(BF) for k in range(count // 2)]
    return [joined[0]] + [swap(joined[k], "tensor", 2 * k) for k in range(1, count // 2)]


def normalize(values, gain):
    wide = values.astype(F32)
    factor = lax.rsqrt(jnp.mean(wide * wide, axis=-1, keepdims=True) + NORM_EPS)
    return (wide * factor * gain.astype(F32)).astype(BF)


def column_of(row):
    count = row.shape[1]
    shape = (count, count)
    same = lax.broadcasted_iota(jnp.int32, shape, 0) == lax.broadcasted_iota(jnp.int32, shape, 1)
    return jnp.sum(jnp.where(same, row, 0.0), axis=1, keepdims=True)


def row_of(column):
    count = column.shape[0]
    shape = (count, count)
    same = lax.broadcasted_iota(jnp.int32, shape, 0) == lax.broadcasted_iota(jnp.int32, shape, 1)
    return jnp.sum(jnp.where(same, column, 0.0), axis=0, keepdims=True)


def picked(row_count, ranks, values):
    rows = lax.broadcasted_iota(jnp.int32, (row_count, ranks.shape[1]), 0).astype(F32)
    return [
        jnp.sum(jnp.where(rows == ranks, value, 0.0), axis=1, keepdims=True) for value in values
    ]


def plan_kernel(sizes, lengths, owners, starts, freqs, *outs):
    groups, count, home_count, slot_rows, sorted_count, cache_rows, rows = sizes
    (
        slots_ref,
        middle_ref,
        own_middle,
        far_pick,
        cos_ref,
        sin_ref,
        home_start,
        home_span,
        home_write,
        home_bounds,
        far_order,
        sort_start,
        sort_span,
        far_write,
        far_bounds,
    ) = outs
    here = lax.axis_index("dp")

    def block(ref, index):
        return ref[:, pl.ds(pl.multiple_of(index * count, LANES), count)]

    def ranks_of(owner, start):
        owner_column, start_column = column_of(owner), column_of(start)
        before = (owner_column == owner) & (start_column < start)
        return jnp.sum(jnp.where(before, 1.0, 0.0), axis=0, keepdims=True)

    def put_ranges(start_ref, span_ref, bounds_ref, start, span):
        start_ref[...] = start.astype(jnp.int32)
        span_ref[...] = span.astype(jnp.int32)
        for tile in range(start.shape[0] // Q_TILE):
            cut = slice(tile * Q_TILE, (tile + 1) * Q_TILE)
            live = span[cut] > 0.0
            low = jnp.min(start[cut]).astype(jnp.int32) // P_TILE
            last = jnp.max(jnp.where(live, start[cut] + span[cut], 0.0)).astype(jnp.int32)
            high = (last + (P_TILE - 1)) // P_TILE
            bounds_ref[0, tile] = jnp.minimum(low, high)
            bounds_ref[1, tile] = high

    my_owner = block(owners, here)
    my_start = block(starts, here).astype(F32)
    my_length = block(lengths, here).astype(F32)
    rank = ranks_of(my_owner.astype(F32), my_start)
    hop = my_owner ^ here
    slot = jnp.where(hop == 0, rank, (hop - 1).astype(F32) * slot_rows + (rank + home_count))
    slots_ref[...] = slot.astype(jnp.int32)
    earlier = column_of(slot) < slot
    place = jnp.sum(jnp.where(earlier, 1.0, 0.0), axis=0, keepdims=True).astype(jnp.int32)
    part = rows // 2
    me = lax.axis_index("tensor")
    middle = (((place // part) ^ me) * part) + place % part
    middle = jnp.where(
        place < count // 2,
        middle,
        (((place - count // 2) // part) ^ me) * part + place % part + count // 2,
    )
    middle_ref[...] = middle
    lane = lax.broadcasted_iota(jnp.int32, (rows, count), 1)
    wanted = lax.broadcasted_iota(jnp.int32, (rows, count), 0) + me * rows
    own_middle[...] = jnp.sum(
        jnp.where(lane == wanted, middle.astype(F32), 0.0), axis=1, keepdims=True
    ).astype(jnp.int32)
    far_count = far_pick.shape[1]
    is_far = jnp.where(hop == 0, 0.0, 1.0)
    shifted = jnp.where(hop == 0, -1.0, slot - home_count)
    taken, offset = picked(far_count, shifted, [is_far, (place - count // 2).astype(F32)])
    far_pick[...] = row_of(jnp.where(taken > 0.0, offset, -1.0)).astype(jnp.int32)
    angles = column_of(my_length) * freqs[...]
    cos_ref[...] = jnp.cos(angles)
    sin_ref[...] = jnp.sin(angles)
    start, span = picked(home_count, slot, [my_start, my_length])
    live = span > 0.0
    start = jnp.where(live, start, float(cache_rows))
    put_ranges(home_start, home_span, home_bounds, start, span)
    home_write[...] = row_of(jnp.where(live, start + span, -1.0)).astype(jnp.int32)

    far = []
    for k in range(1, groups):
        source = here ^ k
        owner = block(owners, source)
        start = block(starts, source).astype(F32)
        rank = ranks_of(owner.astype(F32), start)
        rank = jnp.where(owner == here, rank, -1.0)
        far.append(picked(slot_rows, rank, [start, block(lengths, source).astype(F32)]))
    start = jnp.concatenate([pair[0] for pair in far], axis=0)
    span = jnp.concatenate([pair[1] for pair in far], axis=0)
    live = span > 0.0
    start = jnp.where(live, start, float(cache_rows))
    far_write[...] = row_of(jnp.where(live, start + span, -1.0)).astype(jnp.int32)
    start_row, span_row = row_of(start), row_of(span)
    order = jnp.sum(jnp.where(start < start_row, 1.0, 0.0), axis=0, keepdims=True)
    order = jnp.where(span_row > 0.0, order, -1.0)
    far_order[...] = order.astype(jnp.int32)
    start, span = picked(sorted_count, order, [start_row, span_row])
    start = jnp.where(span > 0.0, start, float(cache_rows))
    put_ranges(sort_start, sort_span, far_bounds, start, span)


def qkv_kernel(piece_count, home_count, slot_rows, hop_count, *refs):
    pieces = refs[:piece_count]
    gain, weights, cosine, sine, slots, middle = refs[piece_count : piece_count + 6]
    home_ref = refs[piece_count + 6]
    out_refs = refs[piece_count + 7 : piece_count + 7 + hop_count]
    token_home, token_far, raw, normed = refs[piece_count + 7 + hop_count :]
    me = lax.axis_index("tensor")
    rows = pieces[0].shape[0]
    for k, piece in enumerate(pieces):
        place = pl.ds(pl.multiple_of((me ^ k) * rows, rows), rows)
        raw[place, :] = piece[...]
        normed[place, :] = normalize(piece[...], gain[...])
    width = weights.shape[2]
    count = normed.shape[0]
    lane = lax.broadcasted_iota(jnp.int32, (count, width), 1)
    low_half = (lane % HD) < HD // 2
    wide = lambda ref: jnp.concatenate([ref[...]] * (width // LANES), axis=1)
    parts = []
    for c in range(3):
        projected = dot(normed[...], weights[c])
        if c < 2:
            ahead = pltpu.roll(projected, width - HD // 2, 1)
            behind = pltpu.roll(projected, HD // 2, 1)
            turned = jnp.where(low_half, -ahead, behind)
            projected = projected * wide(cosine) + turned * wide(sine)
        parts.append(projected.astype(BF))
    packed = jnp.concatenate(parts, axis=1)
    selector = one_hot(home_count + hop_count * slot_rows, slots[...])
    chosen = dot(selector, packed).astype(BF)
    home_ref[...] = chosen[:home_count]
    for k in range(hop_count):
        first = home_count + k * slot_rows
        out_refs[k][...] = chosen[first : first + slot_rows]
    part = rows // 2
    token_home[...] = dot(one_hot(part, middle[...]), raw[...]).astype(BF)
    token_far[...] = dot(one_hot(part, middle[...] - count // 2), raw[...]).astype(BF)


def attend_all(bounds, packed, starts, spans, kv_ref, result, heads, outs):
    width = heads * HD
    rows = Q_TILE
    tiles = packed.shape[0] // rows
    lane_head = lax.broadcasted_iota(jnp.int32, (packed.shape[0], width), 1) // HD
    masks = [lane_head == h for h in range(heads)]
    stack = lambda parts: jnp.concatenate(parts, axis=0)
    query = (packed[:, :width].astype(F32) * (1.0 / math.sqrt(HD))).astype(BF)
    product = query.astype(F32) * packed[:, width : 2 * width].astype(F32)
    owns = [jnp.sum(jnp.where(m, product, 0.0), axis=1, keepdims=True) for m in masks]
    single = [jnp.where(m, query, jnp.zeros_like(query)) for m in masks]
    value = packed[:, 2 * width :].astype(F32)
    tops, totals = [], []
    for tile in range(tiles):
        cut = slice(tile * rows, (tile + 1) * rows)
        own = stack([part[cut] for part in owns])
        stacked = stack([part[cut] for part in single])
        start, span = starts[cut, :], spans[cut, :]

        def advance(step, carry):
            top, total, out = carry
            first = pl.multiple_of(step * P_TILE, P_TILE)
            keys = kv_ref[0, pl.ds(first, P_TILE), :]
            values = kv_ref[1, pl.ds(first, P_TILE), :]
            since = lax.broadcasted_iota(jnp.int32, (rows, P_TILE), 1) + (first - start)
            bias = jnp.where((since >= 0) & (since < span), 0.0, MASK_LOW)
            scores = dot_nt(stacked, keys) + stack([bias] * heads)
            new_top = jnp.maximum(top, jnp.max(scores, axis=1, keepdims=True))
            weights = jnp.exp(scores - new_top)
            factor = jnp.exp(top - new_top)
            total = total * factor + jnp.sum(weights, axis=1, keepdims=True)
            out = out * factor + dot(weights.astype(BF), values)
            return new_top, total, out

        first_carry = (own, jnp.ones_like(own), stack([value[cut]] * heads))
        top, total, out = lax.fori_loop(bounds[0, tile], bounds[1, tile], advance, first_carry)
        tops.append(top)
        totals.append(total)
        outs[tile * heads * rows : (tile + 1) * heads * rows, :] = out
    total = stack(totals)
    log_sum = stack(tops) + jnp.log(total)
    scaled = outs[...] * (1.0 / total)
    pieces = []
    rest = log_sum
    for part in range(3):
        pieces.append(rest.astype(BF).astype(F32))
        rest = rest - pieces[-1]
    lane = lax.broadcasted_iota(jnp.int32, (rows, LANES), 1)
    for tile in range(tiles):
        attended = jnp.zeros((rows, width), F32)
        extra = jnp.zeros((rows, LANES), F32)
        for h in range(heads):
            cut = slice((tile * heads + h) * rows, (tile * heads + h + 1) * rows)
            attended = jnp.where(masks[h][:rows], scaled[cut], attended)
            for part in range(3):
                extra = jnp.where(lane == part * heads + h, pieces[part][cut], extra)
        result[tile * rows : (tile + 1) * rows, :] = jnp.concatenate(
            [attended.astype(BF), extra.astype(BF)], axis=1
        )


def send_middle(attention, weights, keep_ref, send_ref, partial):
    partial[...] = dot(attention, weights[...])
    me = lax.axis_index("tensor")
    part = keep_ref.shape[1]
    for k in range(2 * keep_ref.shape[0]):
        ref = keep_ref if k % 2 == 0 else send_ref
        place = pl.ds(pl.multiple_of((me ^ k) * part, part), part)
        ref[k // 2] = partial[place, :].astype(BF)


def home_kernel(
    heads, bounds, packed, starts, spans, kv_ref, weights, result, keep_ref, send_ref, partial, outs
):
    attend_all(bounds, packed[...], starts, spans, kv_ref, result, heads, outs)
    send_middle(result[:, : heads * HD], weights, keep_ref, send_ref, partial)


def far_kernel(heads, hop_count, sorted_count, bounds, *refs):
    arrived = jnp.concatenate([ref[...] for ref in refs[:hop_count]], axis=0)
    order, starts, spans, kv_ref, _ = refs[hop_count : hop_count + 5]
    outs = refs[hop_count + 5 : 2 * hop_count + 5]
    scratch, state = refs[-2:]
    mover = one_hot(sorted_count, order[...])
    in_order = dot(mover, arrived).astype(BF)
    attend_all(bounds, in_order, starts, spans, kv_ref, scratch, heads, state)
    back = dot_tn(mover, scratch[...]).astype(BF)
    slot_rows = arrived.shape[0] // hop_count
    for k in range(hop_count):
        outs[k][...] = back[k * slot_rows : (k + 1) * slot_rows]


def put_chunks(keep_ref, send_ref, partial, rows):
    me = lax.axis_index("tensor")
    for k in range(partial.shape[0] // rows):
        ref = keep_ref if k % 2 == 0 else send_ref
        ref[k // 2] = partial[pl.ds(pl.multiple_of((me ^ k) * rows, rows), rows), :]


def far_out_kernel(heads, hop_count, slots, far_pick, home, *refs):
    backs = refs[:hop_count]
    weights, log_ref, keep_ref, send_ref, partial = refs[hop_count:]
    width = heads * HD
    far = jnp.concatenate([ref[...] for ref in backs], axis=0)
    placed = dot(one_hot(partial.shape[0], far_pick[...]), far[:, :width]).astype(BF)
    send_middle(placed, weights, keep_ref, send_ref, partial)
    extras = jnp.concatenate([home[:, width:], far[:, width:]], axis=0)
    extra = dot_tn(one_hot(extras.shape[0], slots[...]), extras)
    log_ref[...] = (
        extra + pltpu.roll(extra, LANES - heads, 1) + pltpu.roll(extra, LANES - 2 * heads, 1)
    )


def gate_kernel(piece_count, *refs):
    pieces = refs[:piece_count]
    gain, gate_up, inner_ref = refs[piece_count:]
    values = jnp.concatenate([piece[...] for piece in pieces], axis=0)
    normed = normalize(values, gain[...])
    gate = dot(normed, gate_up[0])
    upward = dot(normed, gate_up[1])
    inner_ref[...] = (gate / (1.0 + jnp.exp(-gate)) * upward).astype(BF)


def down_first_kernel(rows, home, far, middle, down, inner_ref, keep_ref, send_ref, partial):
    half = keep_ref.shape[2]
    both = jnp.concatenate([home[...], far[...]], axis=0)
    inner = dot_tn(one_hot(both.shape[0], middle[...]), both).astype(BF)
    inner_ref[...] = inner
    partial[...] = dot(inner, down[:, :half]).astype(BF)
    put_chunks(keep_ref, send_ref, partial, rows)


def down_second_kernel(rows, inner, down, keep_ref, send_ref, partial):
    half = keep_ref.shape[2]
    partial[...] = dot(inner[...], down[:, half:]).astype(BF)
    put_chunks(keep_ref, send_ref, partial, rows)


def own_rows_kernel(own_middle, *refs):
    pieces = refs[:-1]
    values = jnp.concatenate([piece[...] for piece in pieces], axis=0)
    shape = (own_middle.shape[0], values.shape[0])
    selector = jnp.where(lax.broadcasted_iota(jnp.int32, shape, 1) == own_middle[...], 1.0, 0.0)
    refs[-1][...] = dot(selector.astype(BF), values).astype(BF)


def update_kernel(hop_count, width, home_rows, far_rows, home, *refs):
    far = refs[:hop_count]
    kv_in, kv_out = refs[hop_count:]
    block = kv_in.shape[1]
    position = lax.broadcasted_iota(jnp.int32, (block, 1), 0) + pl.program_id(0) * block
    fresh = jnp.concatenate([home[:, width:]] + [ref[:, width:] for ref in far], axis=0)
    targets = jnp.concatenate([home_rows[...], far_rows[...]], axis=1)
    hit = jnp.where(position == targets, 1.0, 0.0)
    written = jnp.max(hit, axis=1, keepdims=True) > 0.0
    values = dot(hit.astype(BF), fresh).astype(BF)
    kv_out[0] = jnp.where(written, values[:, :width], kv_in[0])
    kv_out[1] = jnp.where(written, values[:, width:], kv_in[1])


def vmem(count):
    return [pl.BlockSpec(memory_space=pltpu.VMEM)] * count


def on_device(
    tokens,
    attn_gain,
    mlp_gain,
    project_in,
    project_out,
    gate_up,
    project_down,
    kv_cache,
    lengths,
    owners,
    cache_start,
):
    groups = lax.axis_size("dp")
    my_index = lax.axis_index("dp")
    tensor_count = lax.axis_size("tensor")
    me = lax.axis_index("tensor")
    rows, model_width = tokens.shape
    request_count = rows * tensor_count
    width = project_in.shape[2]
    heads = width // HD
    cache_rows = kv_cache.shape[1]
    home_count = round_up(request_count - request_count // 2, Q_TILE)
    hops = groups - 1
    capacity = (request_count // 2 + groups - 2) // (groups - 1)
    slot_rows = round_up(capacity, 16)
    far_count = hops * slot_rows
    sorted_count = round_up(min(hops * capacity, far_count), Q_TILE)
    shape = jax.ShapeDtypeStruct
    smem = pl.BlockSpec(memory_space=pltpu.SMEM)
    anywhere = pl.BlockSpec(memory_space=pl.ANY)

    def params(mebibytes):
        return pltpu.CompilerParams(vmem_limit_bytes=mebibytes * 1024 * 1024)

    def cost(flops, bytes_accessed, transcendentals=0):
        return pl.CostEstimate(
            flops=flops, bytes_accessed=bytes_accessed, transcendentals=transcendentals
        )

    ints = lambda *dims: shape(dims, jnp.int32)
    freqs = ROPE_BASE ** (-((jnp.arange(LANES) % (HD // 2)).astype(F32) * 2.0 / HD))
    plan = lambda: pl.pallas_call(
        functools.partial(
            plan_kernel,
            (groups, request_count, home_count, slot_rows, sorted_count, cache_rows, rows),
        ),
        out_shape=[
            ints(1, request_count),
            ints(1, request_count),
            ints(rows, 1),
            ints(1, far_count),
            shape((request_count, LANES), F32),
            shape((request_count, LANES), F32),
            ints(home_count, 1),
            ints(home_count, 1),
            ints(1, home_count),
            ints(2, home_count // Q_TILE),
            ints(1, far_count),
            ints(sorted_count, 1),
            ints(sorted_count, 1),
            ints(1, far_count),
            ints(2, sorted_count // Q_TILE),
        ],
        in_specs=vmem(4),
        out_specs=vmem(9) + [smem] + vmem(4) + [smem],
        compiler_params=params(16),
        cost_estimate=cost(4 * 10**9, 10**6, 10**5),
        name="plan",
    )(lengths[None, :], owners[None, :], cache_start[None, :], freqs[None, :])
    pieces, planned = gather_tensor(tokens, plan)
    (
        slots,
        middle,
        own_middle,
        far_pick,
        cosine,
        sine,
        home_start,
        home_span,
        home_write,
        home_bounds,
        far_order,
        sort_start,
        sort_span,
        far_write,
        far_bounds,
    ) = planned

    part = rows // 2
    middle_count = request_count // 2
    half_count = tensor_count // 2
    packed_outs = pl.pallas_call(
        functools.partial(qkv_kernel, tensor_count, home_count, slot_rows, hops),
        out_shape=[shape((home_count, 3 * width), BF)]
        + [shape((slot_rows, 3 * width), BF)] * hops
        + [shape((part, model_width), BF)] * 2,
        in_specs=vmem(tensor_count + 6),
        out_specs=vmem(3 + hops),
        scratch_shapes=[pltpu.VMEM((request_count, model_width), BF)] * 2,
        compiler_params=params(24),
        name="qkv",
    )(*pieces, attn_gain[None, :], project_in, cosine, sine, slots, middle)
    home_packed = packed_outs[0]
    token_home, token_far = packed_outs[1 + hops :]
    arrived = [swap(packed_outs[k], "dp", k) for k in range(1, groups)]

    out_width = width + LANES
    sums = [shape((half_count, part, model_width), BF)] * 2
    partial_scratch = pltpu.VMEM((middle_count, model_width), F32)
    home_att, keep, send = pl.pallas_call(
        functools.partial(home_kernel, heads),
        out_shape=[shape((home_count, out_width), BF)] + sums,
        in_specs=[smem] + vmem(5),
        out_specs=vmem(3),
        scratch_shapes=[partial_scratch, pltpu.VMEM((home_count * heads, width), F32)],
        compiler_params=params(16),
        cost_estimate=cost(2 * 10**9, 4 * 2**20, 10**6),
        name="home_attention",
    )(home_bounds, home_packed, home_start, home_span, kv_cache, project_out)
    (keep, send), arrived = lax.optimization_barrier(((keep, send), arrived))
    home_sums = reduce_tensor(keep, send)
    far_outs = pl.pallas_call(
        functools.partial(far_kernel, heads, hops, sorted_count),
        out_shape=[shape((slot_rows, out_width), BF)] * hops,
        in_specs=[smem] + vmem(hops + 4) + [anywhere],
        out_specs=vmem(hops),
        scratch_shapes=[
            pltpu.VMEM((sorted_count, out_width), BF),
            pltpu.VMEM((sorted_count * heads, width), F32),
        ],
        compiler_params=params(16),
        cost_estimate=cost(2 * 10**9, 4 * 2**20, 10**6),
        name="far_attention",
    )(far_bounds, *arrived, far_order, sort_start, sort_span, kv_cache, home_att)
    backs = [swap(far_outs[k - 1], "dp", k) for k in range(1, groups)]

    block = 512
    kv_spec = pl.BlockSpec((2, block, width), lambda i: (0, i, 0))
    fixed = lambda array: pl.BlockSpec(array.shape, lambda i: (0,) * array.ndim)
    kv_updated = pl.pallas_call(
        functools.partial(update_kernel, hops, width),
        grid=(cache_rows // block,),
        out_shape=shape(kv_cache.shape, BF),
        in_specs=[fixed(home_write), fixed(far_write), fixed(home_packed)]
        + [fixed(a) for a in arrived]
        + [kv_spec],
        out_specs=kv_spec,
        compiler_params=params(16),
        cost_estimate=cost(2 * 10**9, 8 * 2**20),
        name="cache_update",
    )(home_write, far_write, home_packed, *arrived, kv_cache)

    def add_up(base, sums):
        return (base.astype(F32) + sum(piece.astype(F32) for piece in sums)).astype(BF)

    hidden = gate_up.shape[2]
    gate = lambda pieces, name: pl.pallas_call(
        functools.partial(gate_kernel, tensor_count),
        out_shape=shape((middle_count, hidden), BF),
        in_specs=vmem(tensor_count + 2),
        out_specs=vmem(1)[0],
        compiler_params=params(24),
        cost_estimate=cost(2 * 10**9, 8 * 2**20),
        name=name,
    )(*pieces, mlp_gain[None, :], gate_up)
    home_pieces = gather_tensor(add_up(token_home, home_sums))
    home_inner = gate(home_pieces, "gate_up_home")

    log_sum, keep, send = pl.pallas_call(
        functools.partial(far_out_kernel, heads, hops),
        out_shape=[shape((request_count, LANES), F32)] + sums,
        in_specs=vmem(4 + hops),
        out_specs=vmem(3),
        scratch_shapes=[partial_scratch],
        compiler_params=params(16),
        name="project_out_far",
    )(slots, far_pick, home_att, *backs, project_out)
    log_sum_exp = log_sum[:, :heads]
    far_pieces = gather_tensor(add_up(token_far, reduce_tensor(keep, send)))
    far_inner = gate(far_pieces, "gate_up_far")

    half = model_width // 2
    halves = [shape((half_count, rows, half), BF)] * 2
    row_scratch = [pltpu.VMEM((request_count, half), BF)]
    inner, keep, send = pl.pallas_call(
        functools.partial(down_first_kernel, rows),
        out_shape=[shape((request_count, hidden), BF)] + halves,
        in_specs=vmem(4),
        out_specs=vmem(3),
        scratch_shapes=row_scratch,
        compiler_params=params(16),
        name="down_first",
    )(home_inner, far_inner, middle, project_down)
    sums_first = reduce_tensor(keep, send)
    keep, send = pl.pallas_call(
        functools.partial(down_second_kernel, rows),
        out_shape=halves,
        in_specs=vmem(2),
        out_specs=vmem(2),
        scratch_shapes=row_scratch,
        compiler_params=params(16),
        name="down_second",
    )(inner, project_down)
    sums_second = reduce_tensor(keep, send)
    resid = pl.pallas_call(
        own_rows_kernel,
        out_shape=shape(tokens.shape, BF),
        in_specs=vmem(1 + 2 * tensor_count),
        out_specs=vmem(1)[0],
        compiler_params=params(16),
        name="own_rows",
    )(own_middle, *home_pieces, *far_pieces)
    hidden_states = jnp.concatenate(
        [add_up(resid[:, :half], sums_first), add_up(resid[:, half:], sums_second)], axis=1
    )
    return (hidden_states, log_sum_exp, kv_updated)


def solution(mesh):
    placed = (
        P(("dp", "tensor"), None),
        P(),
        P(),
        P(None, None, "tensor"),
        P("tensor", None),
        P(None, None, "tensor"),
        P("tensor", None),
        P(None, "dp", "tensor"),
        P(),
        P(),
        P(),
    )
    return jax.shard_map(
        on_device,
        mesh=mesh,
        in_specs=placed,
        out_specs=(P(("dp", "tensor"), None), P("dp", "tensor"), P(None, "dp", "tensor")),
        check_vma=False,
    )
```

```python
import functools
import math

import jax
import jax.numpy as jnp
from jax import lax
from jax.experimental import pallas as pl
from jax.experimental.pallas import tpu as pltpu
from jax.sharding import PartitionSpec as P

HD = 64
NORM_EPS = 1e-05
ROPE_BASE = 130000.0
MASK_LOW = -1e30
BF = jnp.bfloat16
F32 = jnp.float32
LANES = 128
Q_TILE = 64
P_TILE = 512


def round_up(count, step):
    return (count + step - 1) // step * step


def row_tiles(count, rows):
    return [slice(at, at + rows) for at in range(0, count, rows)]


def dot(left, right):
    return jnp.dot(left, right, preferred_element_type=F32)


def dot_nt(left, right):
    return lax.dot_general(left, right, (((1,), (1,)), ((), ())), preferred_element_type=F32)


def dot_tn(left, right):
    return lax.dot_general(left, right, (((0,), (0,)), ((), ())), preferred_element_type=F32)


def one_hot(row_count, slots):
    rows = lax.broadcasted_iota(jnp.int32, (row_count, slots.shape[1]), 0)
    return jnp.where(rows == slots, 1.0, 0.0).astype(BF)


def swap(values, axis_name, offset):
    count = lax.axis_size(axis_name)
    return lax.ppermute(values, axis_name, [(i, i ^ offset) for i in range(count)])


def gather_chips(block):
    chips = lax.axis_size("tensor") // 2
    return [block] + [swap(block, "tensor", 2 * k) for k in range(1, chips)]


def gather_cores(blocks):
    return [piece for block in blocks for piece in (block, swap(block, "tensor", 1))]


def gather_tensor(block, beside):
    blocks, done = lax.optimization_barrier((gather_chips(block), beside()))
    return gather_cores(blocks), done


def reduce_chips(keep, send, first):
    came = swap(send, "tensor", 1)
    sums = []
    for i in range(keep.shape[0]):
        joined = (keep[i].astype(F32) + came[i].astype(F32)).astype(BF)
        sums.append(swap(joined, "tensor", 2 * (first + i)) if first + i else joined)
    return sums


def normalize(values, gain):
    wide = values.astype(F32)
    factor = lax.rsqrt(jnp.mean(wide * wide, axis=-1, keepdims=True) + NORM_EPS)
    return (wide * factor * gain.astype(F32)).astype(BF)


def column_of(row):
    count = row.shape[1]
    shape = (count, count)
    same = lax.broadcasted_iota(jnp.int32, shape, 0) == lax.broadcasted_iota(jnp.int32, shape, 1)
    return jnp.sum(jnp.where(same, row, 0.0), axis=1, keepdims=True)


def row_of(column):
    count = column.shape[0]
    shape = (count, count)
    same = lax.broadcasted_iota(jnp.int32, shape, 0) == lax.broadcasted_iota(jnp.int32, shape, 1)
    return jnp.sum(jnp.where(same, column, 0.0), axis=0, keepdims=True)


def picked(row_count, ranks, values):
    rows = lax.broadcasted_iota(jnp.int32, (row_count, ranks.shape[1]), 0).astype(F32)
    return [
        jnp.sum(jnp.where(rows == ranks, value, 0.0), axis=1, keepdims=True) for value in values
    ]


def plan_kernel(sizes, lengths, owners, starts, freqs, *outs):
    groups, count, home_count, slot_rows, cache_rows, rows = sizes
    (
        slots_ref,
        middle_ref,
        own_order,
        far_pick,
        cos_ref,
        sin_ref,
        home_start,
        home_span,
        home_write,
        home_bounds,
        far_start,
        far_span,
        far_write,
        far_bounds,
    ) = outs
    here = lax.axis_index("dp")

    def block(ref, index):
        return ref[:, pl.ds(pl.multiple_of(index * count, LANES), count)]

    def ranks_of(owner, start):
        owner_column, start_column = column_of(owner), column_of(start)
        before = (owner_column == owner) & (start_column < start)
        return jnp.sum(jnp.where(before, 1.0, 0.0), axis=0, keepdims=True)

    def put_ranges(start_ref, span_ref, bounds_ref, start, span, tile_rows):
        start_ref[...] = start.astype(jnp.int32)
        span_ref[...] = span.astype(jnp.int32)
        for tile, cut in enumerate(row_tiles(start.shape[0], tile_rows)):
            live = span[cut] > 0.0
            low = jnp.min(start[cut]).astype(jnp.int32) // P_TILE
            last = jnp.max(jnp.where(live, start[cut] + span[cut], 0.0)).astype(jnp.int32)
            high = (last + (P_TILE - 1)) // P_TILE
            bounds_ref[0, tile] = jnp.minimum(low, high)
            bounds_ref[1, tile] = high

    my_owner = block(owners, here)
    my_start = block(starts, here).astype(F32)
    my_length = block(lengths, here).astype(F32)
    rank = ranks_of(my_owner.astype(F32), my_start)
    hop = my_owner ^ here
    slot = jnp.where(hop == 0, rank, (hop - 1).astype(F32) * slot_rows + (rank + home_count))
    slots_ref[...] = slot.astype(jnp.int32)
    earlier = column_of(slot) < slot
    place = jnp.sum(jnp.where(earlier, 1.0, 0.0), axis=0, keepdims=True).astype(jnp.int32)
    part = rows // 2
    me = lax.axis_index("tensor")
    middle = (((place // part) ^ me) * part) + place % part
    middle = jnp.where(
        place < count // 2,
        middle,
        (((place - count // 2) // part) ^ me) * part + place % part + count // 2,
    )
    middle_ref[...] = middle
    request = lax.broadcasted_iota(jnp.int32, (1, count), 1)
    relative = (((request // rows) ^ me) * rows + request % rows).astype(F32)
    own_order[...] = row_of(picked(count, relative, [middle.astype(F32)])[0]).astype(jnp.int32)
    far_count = far_pick.shape[1]
    is_far = jnp.where(hop == 0, 0.0, 1.0)
    shifted = jnp.where(hop == 0, -1.0, slot - home_count)
    taken, offset = picked(far_count, shifted, [is_far, (place - count // 2).astype(F32)])
    far_pick[...] = row_of(jnp.where(taken > 0.0, offset, -1.0)).astype(jnp.int32)
    angles = column_of(my_length) * freqs[...]
    cos_ref[...] = jnp.cos(angles)
    sin_ref[...] = jnp.sin(angles)
    start, span = picked(home_count, slot, [my_start, my_length])
    live = span > 0.0
    start = jnp.where(live, start, float(cache_rows))
    put_ranges(home_start, home_span, home_bounds, start, span, Q_TILE)
    home_write[...] = row_of(jnp.where(live, start + span, -1.0)).astype(jnp.int32)

    far = []
    for k in range(1, groups):
        source = here ^ k
        owner = block(owners, source)
        start = block(starts, source).astype(F32)
        rank = ranks_of(owner.astype(F32), start)
        rank = jnp.where(owner == here, rank, -1.0)
        far.append(picked(slot_rows, rank, [start, block(lengths, source).astype(F32)]))
    start = jnp.concatenate([pair[0] for pair in far], axis=0)
    span = jnp.concatenate([pair[1] for pair in far], axis=0)
    live = span > 0.0
    start = jnp.where(live, start, float(cache_rows))
    far_write[...] = row_of(jnp.where(live, start + span, -1.0)).astype(jnp.int32)
    put_ranges(far_start, far_span, far_bounds, start, span, slot_rows)


def qkv_kernel(piece_count, home_count, slot_rows, hop_count, *refs):
    pieces = refs[:piece_count]
    gain, weights, cosine, sine, slots, middle = refs[piece_count : piece_count + 6]
    home_ref = refs[piece_count + 6]
    out_refs = refs[piece_count + 7 : piece_count + 7 + hop_count]
    token_home, token_far, raw, normed = refs[piece_count + 7 + hop_count :]
    me = lax.axis_index("tensor")
    rows = pieces[0].shape[0]
    for k, piece in enumerate(pieces):
        place = pl.ds(pl.multiple_of((me ^ k) * rows, rows), rows)
        raw[place, :] = piece[...]
        normed[place, :] = normalize(piece[...], gain[...])
    width = weights.shape[2]
    count = normed.shape[0]
    lane = lax.broadcasted_iota(jnp.int32, (count, width), 1)
    low_half = (lane % HD) < HD // 2
    wide = lambda ref: jnp.concatenate([ref[...]] * (width // LANES), axis=1)
    parts = []
    for c in range(3):
        projected = dot(normed[...], weights[c])
        if c < 2:
            ahead = pltpu.roll(projected, width - HD // 2, 1)
            behind = pltpu.roll(projected, HD // 2, 1)
            turned = jnp.where(low_half, -ahead, behind)
            projected = projected * wide(cosine) + turned * wide(sine)
        parts.append(projected.astype(BF))
    packed = jnp.concatenate(parts, axis=1)
    selector = one_hot(home_count + hop_count * slot_rows, slots[...])
    chosen = dot(selector, packed).astype(BF)
    home_ref[...] = chosen[:home_count]
    for k in range(hop_count):
        first = home_count + k * slot_rows
        out_refs[k][...] = chosen[first : first + slot_rows]
    part = rows // 2
    token_home[...] = dot(one_hot(part, middle[...]), raw[...]).astype(BF)
    token_far[...] = dot(one_hot(part, middle[...] - count // 2), raw[...]).astype(BF)


def attend_all(bounds, packed, starts, spans, kv_ref, result, heads, outs, tile_rows):
    width = heads * HD
    tiles = row_tiles(packed.shape[0], tile_rows)
    lane_head = lax.broadcasted_iota(jnp.int32, (packed.shape[0], width), 1) // HD
    masks = [lane_head == h for h in range(heads)]
    stack = lambda parts: jnp.concatenate(parts, axis=0)
    query = (packed[:, :width].astype(F32) * (1.0 / math.sqrt(HD))).astype(BF)
    product = query.astype(F32) * packed[:, width : 2 * width].astype(F32)
    owns = [jnp.sum(jnp.where(m, product, 0.0), axis=1, keepdims=True) for m in masks]
    single = [jnp.where(m, query, jnp.zeros_like(query)) for m in masks]
    value = packed[:, 2 * width :].astype(F32)
    tops, totals = [], []
    for tile, cut in enumerate(tiles):
        rows = cut.stop - cut.start
        own = stack([part[cut] for part in owns])
        stacked = stack([part[cut] for part in single])
        start, span = starts[cut, :], spans[cut, :]

        def advance(step, carry, rows=rows, start=start, span=span, stacked=stacked):
            top, total, out = carry
            first = pl.multiple_of(step * P_TILE, P_TILE)
            keys = kv_ref[0, pl.ds(first, P_TILE), :]
            values = kv_ref[1, pl.ds(first, P_TILE), :]
            since = lax.broadcasted_iota(jnp.int32, (rows, P_TILE), 1) + (first - start)
            bias = jnp.where((since >= 0) & (since < span), 0.0, MASK_LOW)
            scores = dot_nt(stacked, keys) + stack([bias] * heads)
            new_top = jnp.maximum(top, jnp.max(scores, axis=1, keepdims=True))
            weights = jnp.exp(scores - new_top)
            factor = jnp.exp(top - new_top)
            total = total * factor + jnp.sum(weights, axis=1, keepdims=True)
            out = out * factor + dot(weights.astype(BF), values)
            return new_top, total, out

        first_carry = (own, jnp.ones_like(own), stack([value[cut]] * heads))
        top, total, out = lax.fori_loop(bounds[0, tile], bounds[1, tile], advance, first_carry)
        tops.append(top)
        totals.append(total)
        outs[cut.start * heads : cut.stop * heads, :] = out
    total = stack(totals)
    log_sum = stack(tops) + jnp.log(total)
    scaled = outs[...] * (1.0 / total)
    pieces = []
    rest = log_sum
    for part in range(3):
        pieces.append(rest.astype(BF).astype(F32))
        rest = rest - pieces[-1]
    for tile in tiles:
        rows = tile.stop - tile.start
        lane = lax.broadcasted_iota(jnp.int32, (rows, LANES), 1)
        attended = jnp.zeros((rows, width), F32)
        extra = jnp.zeros((rows, LANES), F32)
        for h in range(heads):
            first = tile.start * heads + h * rows
            cut = slice(first, first + rows)
            attended = jnp.where(masks[h][:rows], scaled[cut], attended)
            for part in range(3):
                extra = jnp.where(lane == part * heads + h, pieces[part][cut], extra)
        result[tile, :] = jnp.concatenate(
            [attended.astype(BF), extra.astype(BF)], axis=1
        )


def send_middle(attention, weights, keep_ref, send_ref, partial):
    partial[...] = dot(attention, weights[...])
    me = lax.axis_index("tensor")
    part = keep_ref.shape[1]
    for k in range(2 * keep_ref.shape[0]):
        ref = keep_ref if k % 2 == 0 else send_ref
        place = pl.ds(pl.multiple_of((me ^ k) * part, part), part)
        ref[k // 2] = partial[place, :].astype(BF)


def home_kernel(
    heads, bounds, packed, starts, spans, kv_ref, weights, result, keep_ref, send_ref, partial, outs
):
    attend_all(bounds, packed[...], starts, spans, kv_ref, result, heads, outs, Q_TILE)
    send_middle(result[:, : heads * HD], weights, keep_ref, send_ref, partial)


def far_kernel(heads, hop_count, bounds, *refs):
    arrived = jnp.concatenate([ref[...] for ref in refs[:hop_count]], axis=0)
    starts, spans, kv_ref, _ = refs[hop_count : hop_count + 4]
    *outs, result, state = refs[hop_count + 4 :]
    rows = arrived.shape[0] // hop_count
    attend_all(bounds, arrived, starts, spans, kv_ref, result, heads, state, rows)
    for k in range(hop_count):
        outs[k][...] = result[k * rows : (k + 1) * rows, :]


def far_out_kernel(heads, hop_count, slots, far_pick, home, *refs):
    backs = refs[:hop_count]
    weights, log_ref, keep_ref, send_ref, partial = refs[hop_count:]
    width = heads * HD
    far = jnp.concatenate([ref[...] for ref in backs], axis=0)
    placed = dot(one_hot(partial.shape[0], far_pick[...]), far[:, :width]).astype(BF)
    send_middle(placed, weights, keep_ref, send_ref, partial)
    extras = jnp.concatenate([home[:, width:], far[:, width:]], axis=0)
    extra = dot_tn(one_hot(extras.shape[0], slots[...]), extras)
    log_ref[...] = (
        extra + pltpu.roll(extra, LANES - heads, 1) + pltpu.roll(extra, LANES - 2 * heads, 1)
    )


def gate_kernel(piece_count, *refs):
    pieces = refs[:piece_count]
    gain, gate_up, inner_ref = refs[piece_count:]
    values = jnp.concatenate([piece[...] for piece in pieces], axis=0)
    normed = normalize(values, gain[...])
    gate = dot(normed, gate_up[0])
    upward = dot(normed, gate_up[1])
    inner_ref[...] = (gate / (1.0 + jnp.exp(-gate)) * upward).astype(BF)


def send_rows(partial, rows, keep_ref, send_ref):
    for k in range(partial.shape[0] // rows):
        ref = keep_ref if k % 2 == 0 else send_ref
        ref[k // 2] = partial[k * rows : (k + 1) * rows]


def down_first_kernel(rows, home, far, order, down, rest_ref, keep_ref, send_ref):
    both = jnp.concatenate([home[...], far[...]], axis=0)
    inner = dot_tn(one_hot(both.shape[0], order[...]), both).astype(BF)
    half = rest_ref.shape[0]
    rest_ref[...] = inner[:half]
    send_rows(dot(inner[half:], down[...]).astype(BF), rows, keep_ref, send_ref)


def down_second_kernel(rows, inner, down, keep_ref, send_ref):
    send_rows(dot(inner[...], down[...]).astype(BF), rows, keep_ref, send_ref)


def own_rows_kernel(order, *refs):
    pieces = refs[:-1]
    values = jnp.concatenate([piece[...] for piece in pieces], axis=0)
    rows = refs[-1].shape[0]
    chosen = dot_tn(one_hot(values.shape[0], order[...]), values)
    refs[-1][...] = chosen[:rows].astype(BF)


def update_kernel(hop_count, width, home_rows, far_rows, home, *refs):
    far = refs[:hop_count]
    kv_in, kv_out = refs[hop_count:]
    block = kv_in.shape[1]
    position = lax.broadcasted_iota(jnp.int32, (block, 1), 0) + pl.program_id(0) * block
    fresh = jnp.concatenate([home[:, width:]] + [ref[:, width:] for ref in far], axis=0)
    targets = jnp.concatenate([home_rows[...], far_rows[...]], axis=1)
    hit = jnp.where(position == targets, 1.0, 0.0)
    written = jnp.max(hit, axis=1, keepdims=True) > 0.0
    values = dot(hit.astype(BF), fresh).astype(BF)
    kv_out[0] = jnp.where(written, values[:, :width], kv_in[0])
    kv_out[1] = jnp.where(written, values[:, width:], kv_in[1])


def vmem(count):
    return [pl.BlockSpec(memory_space=pltpu.VMEM)] * count


def on_device(
    tokens,
    attn_gain,
    mlp_gain,
    project_in,
    project_out,
    gate_up,
    project_down,
    kv_cache,
    lengths,
    owners,
    cache_start,
):
    groups = lax.axis_size("dp")
    my_index = lax.axis_index("dp")
    tensor_count = lax.axis_size("tensor")
    me = lax.axis_index("tensor")
    rows, model_width = tokens.shape
    request_count = rows * tensor_count
    width = project_in.shape[2]
    heads = width // HD
    cache_rows = kv_cache.shape[1]
    home_count = round_up(request_count - request_count // 2, Q_TILE)
    hops = groups - 1
    capacity = (request_count // 2 + groups - 2) // (groups - 1)
    slot_rows = round_up(capacity, 16)
    far_count = hops * slot_rows
    shape = jax.ShapeDtypeStruct
    smem = pl.BlockSpec(memory_space=pltpu.SMEM)
    anywhere = pl.BlockSpec(memory_space=pl.ANY)

    def params(mebibytes):
        return pltpu.CompilerParams(vmem_limit_bytes=mebibytes * 1024 * 1024)

    def cost(flops, bytes_accessed, transcendentals=0):
        return pl.CostEstimate(
            flops=flops, bytes_accessed=bytes_accessed, transcendentals=transcendentals
        )

    ints = lambda *dims: shape(dims, jnp.int32)
    freqs = ROPE_BASE ** (-((jnp.arange(LANES) % (HD // 2)).astype(F32) * 2.0 / HD))
    plan = lambda: pl.pallas_call(
        functools.partial(
            plan_kernel,
            (groups, request_count, home_count, slot_rows, cache_rows, rows),
        ),
        out_shape=[
            ints(1, request_count),
            ints(1, request_count),
            ints(1, request_count),
            ints(1, far_count),
            shape((request_count, LANES), F32),
            shape((request_count, LANES), F32),
            ints(home_count, 1),
            ints(home_count, 1),
            ints(1, home_count),
            ints(2, home_count // Q_TILE),
            ints(far_count, 1),
            ints(far_count, 1),
            ints(1, far_count),
            ints(2, hops),
        ],
        in_specs=vmem(4),
        out_specs=vmem(9) + [smem] + vmem(3) + [smem],
        compiler_params=params(16),
        cost_estimate=cost(4 * 10**9, 10**6, 10**5),
        name="plan",
    )(lengths[None, :], owners[None, :], cache_start[None, :], freqs[None, :])
    pieces, planned = gather_tensor(tokens, plan)
    (
        slots,
        middle,
        own_order,
        far_pick,
        cosine,
        sine,
        home_start,
        home_span,
        home_write,
        home_bounds,
        far_start,
        far_span,
        far_write,
        far_bounds,
    ) = planned

    part = rows // 2
    middle_count = request_count // 2
    half_count = tensor_count // 2
    packed_outs = pl.pallas_call(
        functools.partial(qkv_kernel, tensor_count, home_count, slot_rows, hops),
        out_shape=[shape((home_count, 3 * width), BF)]
        + [shape((slot_rows, 3 * width), BF)] * hops
        + [shape((part, model_width), BF)] * 2,
        in_specs=vmem(tensor_count + 6),
        out_specs=vmem(3 + hops),
        scratch_shapes=[pltpu.VMEM((request_count, model_width), BF)] * 2,
        compiler_params=params(16),
        name="qkv",
    )(*pieces, attn_gain[None, :], project_in, cosine, sine, slots, middle)
    home_packed = packed_outs[0]
    token_home, token_far = packed_outs[1 + hops :]
    arrived = [swap(packed_outs[k], "dp", k) for k in range(1, groups)]

    out_width = width + LANES
    sums = [shape((half_count, part, model_width), BF)] * 2
    partial_scratch = pltpu.VMEM((middle_count, model_width), F32)
    home_att, keep, send = pl.pallas_call(
        functools.partial(home_kernel, heads),
        out_shape=[shape((home_count, out_width), BF)] + sums,
        in_specs=[smem] + vmem(5),
        out_specs=vmem(3),
        scratch_shapes=[partial_scratch, pltpu.VMEM((home_count * heads, width), F32)],
        compiler_params=params(16),
        cost_estimate=cost(2 * 10**9, 4 * 2**20, 10**6),
        name="home_attention",
    )(home_bounds, home_packed, home_start, home_span, kv_cache, project_out)
    (keep, send), arrived = lax.optimization_barrier(((keep, send), arrived))
    home_sums = reduce_chips(keep, send, 0)
    far_outs = pl.pallas_call(
        functools.partial(far_kernel, heads, hops),
        out_shape=[shape((slot_rows, out_width), BF)] * hops,
        in_specs=[smem] + vmem(hops + 3) + [anywhere],
        out_specs=vmem(hops),
        scratch_shapes=[
            pltpu.VMEM((far_count, out_width), BF),
            pltpu.VMEM((far_count * heads, width), F32),
        ],
        compiler_params=params(16),
        cost_estimate=cost(2 * 10**9, 4 * 2**20, 10**6),
        name="far_attention",
    )(far_bounds, *arrived, far_start, far_span, kv_cache, home_att)
    backs = [swap(far_outs[k - 1], "dp", k) for k in range(1, groups)]

    block = 512
    kv_spec = pl.BlockSpec((2, block, width), lambda i: (0, i, 0))
    fixed = lambda array: pl.BlockSpec(array.shape, lambda i: (0,) * array.ndim)
    kv_updated = pl.pallas_call(
        functools.partial(update_kernel, hops, width),
        grid=(cache_rows // block,),
        out_shape=shape(kv_cache.shape, BF),
        in_specs=[fixed(home_write), fixed(far_write), fixed(home_packed)]
        + [fixed(a) for a in arrived]
        + [kv_spec],
        out_specs=kv_spec,
        compiler_params=params(16),
        cost_estimate=cost(2 * 10**9, 8 * 2**20),
        name="cache_update",
    )(home_write, far_write, home_packed, *arrived, kv_cache)

    def add_up(base, sums):
        return (base.astype(F32) + sum(piece.astype(F32) for piece in sums)).astype(BF)

    hidden = gate_up.shape[2]
    gate = lambda pieces, name: pl.pallas_call(
        functools.partial(gate_kernel, tensor_count),
        out_shape=shape((middle_count, hidden), BF),
        in_specs=vmem(tensor_count + 2),
        out_specs=vmem(1)[0],
        compiler_params=params(16),
        cost_estimate=cost(2 * 10**9, 8 * 2**20),
        name=name,
    )(*pieces, mlp_gain[None, :], gate_up)
    backs, home_sums = lax.optimization_barrier((backs, home_sums))
    home_far_chips = gather_chips(add_up(token_home, home_sums))

    log_sum, keep, send = pl.pallas_call(
        functools.partial(far_out_kernel, heads, hops),
        out_shape=[shape((request_count, LANES), F32)] + sums,
        in_specs=vmem(4 + hops),
        out_specs=vmem(3),
        scratch_shapes=[partial_scratch],
        compiler_params=params(16),
        name="project_out_far",
    )(slots, far_pick, home_att, *backs, project_out)
    log_sum_exp = log_sum[:, :heads]
    far_sums, home_far_chips = lax.optimization_barrier(
        (reduce_chips(keep, send, 0), home_far_chips)
    )
    home_pieces = gather_cores(home_far_chips)
    far_pieces, home_inner = gather_tensor(
        add_up(token_far, far_sums), lambda: gate(home_pieces, "gate_up_home")
    )
    far_inner = gate(far_pieces, "gate_up_far")

    near = half_count // 2
    quarters = [shape((near, rows, model_width), BF)] * 2
    rest, keep, send = pl.pallas_call(
        functools.partial(down_first_kernel, rows),
        out_shape=[shape((middle_count, hidden), BF)] + quarters,
        in_specs=vmem(4),
        out_specs=vmem(3),
        compiler_params=params(16),
        name="down_first",
    )(home_inner, far_inner, own_order, project_down)
    down_sums = reduce_chips(keep, send, near)
    keep, send = pl.pallas_call(
        functools.partial(down_second_kernel, rows),
        out_shape=quarters,
        in_specs=vmem(2),
        out_specs=vmem(2),
        compiler_params=params(16),
        name="down_second",
    )(rest, project_down)
    down_sums += reduce_chips(keep, send, 0)
    resid = pl.pallas_call(
        own_rows_kernel,
        out_shape=shape(tokens.shape, BF),
        in_specs=vmem(1 + 2 * tensor_count),
        out_specs=vmem(1)[0],
        compiler_params=params(16),
        name="own_rows",
    )(own_order, *home_pieces, *far_pieces)
    hidden_states = add_up(resid, down_sums)
    return (hidden_states, log_sum_exp, kv_updated)


def solution(mesh):
    placed = (
        P(("dp", "tensor"), None),
        P(),
        P(),
        P(None, None, "tensor"),
        P("tensor", None),
        P(None, None, "tensor"),
        P("tensor", None),
        P(None, "dp", "tensor"),
        P(),
        P(),
        P(),
    )
    return jax.shard_map(
        on_device,
        mesh=mesh,
        in_specs=placed,
        out_specs=(P(("dp", "tensor"), None), P("dp", "tensor"), P(None, "dp", "tensor")),
        check_vma=False,
    )
```

```python
import functools
import math

import jax
import jax.numpy as jnp
from jax import lax
from jax.experimental import pallas as pl
from jax.experimental.pallas import tpu as pltpu
from jax.sharding import PartitionSpec as P

HD = 64
NORM_EPS = 1e-05
ROPE_BASE = 130000.0
MASK_LOW = -1e30
BF = jnp.bfloat16
F32 = jnp.float32
LANES = 128
Q_TILE = 64
P_TILE = 512


def round_up(count, step):
    return (count + step - 1) // step * step


def row_tiles(count, rows):
    return [slice(at, at + rows) for at in range(0, count, rows)]


def dot(left, right):
    return jnp.dot(left, right, preferred_element_type=F32)


def dot_nt(left, right):
    return lax.dot_general(left, right, (((1,), (1,)), ((), ())), preferred_element_type=F32)


def dot_tn(left, right):
    return lax.dot_general(left, right, (((0,), (0,)), ((), ())), preferred_element_type=F32)


def one_hot(row_count, slots):
    rows = lax.broadcasted_iota(jnp.int32, (row_count, slots.shape[1]), 0)
    return jnp.where(rows == slots, 1.0, 0.0).astype(BF)


def swap(values, axis_name, offset):
    count = lax.axis_size(axis_name)
    return lax.ppermute(values, axis_name, [(i, i ^ offset) for i in range(count)])


def gather_chips(block):
    chips = lax.axis_size("tensor") // 2
    return [block] + [swap(block, "tensor", 2 * k) for k in range(1, chips)]


def gather_cores(blocks):
    return [piece for block in blocks for piece in (block, swap(block, "tensor", 1))]


def gather_tensor(block, beside):
    blocks, done = lax.optimization_barrier((gather_chips(block), beside()))
    return gather_cores(blocks), done


def reduce_chips(keep, send, first):
    came = swap(send, "tensor", 1)
    sums = []
    for i in range(keep.shape[0]):
        joined = (keep[i].astype(F32) + came[i].astype(F32)).astype(BF)
        sums.append(swap(joined, "tensor", 2 * (first + i)) if first + i else joined)
    return sums


def normalize(values, gain):
    wide = values.astype(F32)
    factor = lax.rsqrt(jnp.mean(wide * wide, axis=-1, keepdims=True) + NORM_EPS)
    return (wide * factor * gain.astype(F32)).astype(BF)


def column_of(row):
    count = row.shape[1]
    shape = (count, count)
    same = lax.broadcasted_iota(jnp.int32, shape, 0) == lax.broadcasted_iota(jnp.int32, shape, 1)
    return jnp.sum(jnp.where(same, row, 0.0), axis=1, keepdims=True)


def row_of(column):
    count = column.shape[0]
    shape = (count, count)
    same = lax.broadcasted_iota(jnp.int32, shape, 0) == lax.broadcasted_iota(jnp.int32, shape, 1)
    return jnp.sum(jnp.where(same, column, 0.0), axis=0, keepdims=True)


def picked(row_count, ranks, values):
    rows = lax.broadcasted_iota(jnp.int32, (row_count, ranks.shape[1]), 0).astype(F32)
    return [
        jnp.sum(jnp.where(rows == ranks, value, 0.0), axis=1, keepdims=True) for value in values
    ]


def plan_kernel(sizes, lengths, owners, starts, freqs, *outs):
    groups, count, home_count, slot_rows, cache_rows, rows = sizes
    (
        slots_ref,
        middle_ref,
        own_order,
        far_pick,
        cos_ref,
        sin_ref,
        home_start,
        home_span,
        home_write,
        home_bounds,
        far_start,
        far_span,
        far_write,
        far_bounds,
    ) = outs
    here = lax.axis_index("dp")

    def block(ref, index):
        return ref[:, pl.ds(pl.multiple_of(index * count, LANES), count)]

    def ranks_of(owner, start):
        owner_column, start_column = column_of(owner), column_of(start)
        before = (owner_column == owner) & (start_column < start)
        return jnp.sum(jnp.where(before, 1.0, 0.0), axis=0, keepdims=True)

    def put_ranges(start_ref, span_ref, bounds_ref, start, span, tile_rows):
        start_ref[...] = start.astype(jnp.int32)
        span_ref[...] = span.astype(jnp.int32)
        for tile, cut in enumerate(row_tiles(start.shape[0], tile_rows)):
            live = span[cut] > 0.0
            low = jnp.min(start[cut]).astype(jnp.int32) // P_TILE
            last = jnp.max(jnp.where(live, start[cut] + span[cut], 0.0)).astype(jnp.int32)
            high = (last + (P_TILE - 1)) // P_TILE
            bounds_ref[0, tile] = jnp.minimum(low, high)
            bounds_ref[1, tile] = high

    my_owner = block(owners, here)
    my_start = block(starts, here).astype(F32)
    my_length = block(lengths, here).astype(F32)
    rank = ranks_of(my_owner.astype(F32), my_start)
    hop = my_owner ^ here
    slot = jnp.where(hop == 0, rank, (hop - 1).astype(F32) * slot_rows + (rank + home_count))
    slots_ref[...] = slot.astype(jnp.int32)
    earlier = column_of(slot) < slot
    place = jnp.sum(jnp.where(earlier, 1.0, 0.0), axis=0, keepdims=True).astype(jnp.int32)
    part = rows // 2
    me = lax.axis_index("tensor")
    middle = (((place // part) ^ me) * part) + place % part
    middle = jnp.where(
        place < count // 2,
        middle,
        (((place - count // 2) // part) ^ me) * part + place % part + count // 2,
    )
    middle_ref[...] = middle
    request = lax.broadcasted_iota(jnp.int32, (1, count), 1)
    relative = (((request // rows) ^ me) * rows + request % rows).astype(F32)
    own_order[...] = row_of(picked(count, relative, [middle.astype(F32)])[0]).astype(jnp.int32)
    far_count = far_pick.shape[1]
    is_far = jnp.where(hop == 0, 0.0, 1.0)
    shifted = jnp.where(hop == 0, -1.0, slot - home_count)
    taken, offset = picked(far_count, shifted, [is_far, (place - count // 2).astype(F32)])
    far_pick[...] = row_of(jnp.where(taken > 0.0, offset, -1.0)).astype(jnp.int32)
    angles = column_of(my_length) * freqs[...]
    cos_ref[...] = jnp.cos(angles)
    sin_ref[...] = jnp.sin(angles)
    start, span = picked(home_count, slot, [my_start, my_length])
    live = span > 0.0
    start = jnp.where(live, start, float(cache_rows))
    put_ranges(home_start, home_span, home_bounds, start, span, Q_TILE)
    home_write[...] = row_of(jnp.where(live, start + span, -1.0)).astype(jnp.int32)

    far = []
    for k in range(1, groups):
        source = here ^ k
        owner = block(owners, source)
        start = block(starts, source).astype(F32)
        rank = ranks_of(owner.astype(F32), start)
        rank = jnp.where(owner == here, rank, -1.0)
        far.append(picked(slot_rows, rank, [start, block(lengths, source).astype(F32)]))
    start = jnp.concatenate([pair[0] for pair in far], axis=0)
    span = jnp.concatenate([pair[1] for pair in far], axis=0)
    live = span > 0.0
    start = jnp.where(live, start, float(cache_rows))
    far_write[...] = row_of(jnp.where(live, start + span, -1.0)).astype(jnp.int32)
    put_ranges(far_start, far_span, far_bounds, start, span, slot_rows)


def qkv_kernel(piece_count, home_count, slot_rows, hop_count, *refs):
    pieces = refs[:piece_count]
    gain, weights, cosine, sine, slots, middle = refs[piece_count : piece_count + 6]
    home_ref = refs[piece_count + 6]
    out_refs = refs[piece_count + 7 : piece_count + 7 + hop_count]
    token_home, token_far, raw, normed = refs[piece_count + 7 + hop_count :]
    me = lax.axis_index("tensor")
    rows = pieces[0].shape[0]
    for k, piece in enumerate(pieces):
        place = pl.ds(pl.multiple_of((me ^ k) * rows, rows), rows)
        raw[place, :] = piece[...]
        normed[place, :] = normalize(piece[...], gain[...])
    width = weights.shape[2]
    count = normed.shape[0]
    lane = lax.broadcasted_iota(jnp.int32, (count, width), 1)
    low_half = (lane % HD) < HD // 2
    wide = lambda ref: jnp.concatenate([ref[...]] * (width // LANES), axis=1)
    parts = []
    for c in range(3):
        projected = dot(normed[...], weights[c])
        if c < 2:
            ahead = pltpu.roll(projected, width - HD // 2, 1)
            behind = pltpu.roll(projected, HD // 2, 1)
            turned = jnp.where(low_half, -ahead, behind)
            projected = projected * wide(cosine) + turned * wide(sine)
        parts.append(projected.astype(BF))
    packed = jnp.concatenate(parts, axis=1)
    selector = one_hot(home_count + hop_count * slot_rows, slots[...])
    chosen = dot(selector, packed).astype(BF)
    home_ref[...] = chosen[:home_count]
    for k in range(hop_count):
        first = home_count + k * slot_rows
        out_refs[k][...] = chosen[first : first + slot_rows]
    part = rows // 2
    token_home[...] = dot(one_hot(part, middle[...]), raw[...]).astype(BF)
    token_far[...] = dot(one_hot(part, middle[...] - count // 2), raw[...]).astype(BF)


def attend_all(bounds, packed, starts, spans, kv_ref, result, heads, outs, tile_rows):
    width = heads * HD
    tiles = row_tiles(packed.shape[0], tile_rows)
    lane_head = lax.broadcasted_iota(jnp.int32, (packed.shape[0], width), 1) // HD
    masks = [lane_head == h for h in range(heads)]
    stack = lambda parts: jnp.concatenate(parts, axis=0)
    query = (packed[:, :width].astype(F32) * (1.0 / math.sqrt(HD))).astype(BF)
    product = query.astype(F32) * packed[:, width : 2 * width].astype(F32)
    owns = [jnp.sum(jnp.where(m, product, 0.0), axis=1, keepdims=True) for m in masks]
    single = [jnp.where(m, query, jnp.zeros_like(query)) for m in masks]
    value = packed[:, 2 * width :].astype(F32)
    tops, totals = [], []
    for tile, cut in enumerate(tiles):
        rows = cut.stop - cut.start
        own = stack([part[cut] for part in owns])
        stacked = stack([part[cut] for part in single])
        start, span = starts[cut, :], spans[cut, :]

        def advance(step, carry, rows=rows, start=start, span=span, stacked=stacked):
            top, total, out = carry
            first = pl.multiple_of(step * P_TILE, P_TILE)
            keys = kv_ref[0, pl.ds(first, P_TILE), :]
            values = kv_ref[1, pl.ds(first, P_TILE), :]
            since = lax.broadcasted_iota(jnp.int32, (rows, P_TILE), 1) + (first - start)
            bias = jnp.where((since >= 0) & (since < span), 0.0, MASK_LOW)
            scores = dot_nt(stacked, keys) + stack([bias] * heads)
            new_top = jnp.maximum(top, jnp.max(scores, axis=1, keepdims=True))
            weights = jnp.exp(scores - new_top)
            factor = jnp.exp(top - new_top)
            total = total * factor + jnp.sum(weights, axis=1, keepdims=True)
            out = out * factor + dot(weights.astype(BF), values)
            return new_top, total, out

        first_carry = (own, jnp.ones_like(own), stack([value[cut]] * heads))
        top, total, out = lax.fori_loop(bounds[0, tile], bounds[1, tile], advance, first_carry)
        tops.append(top)
        totals.append(total)
        outs[cut.start * heads : cut.stop * heads, :] = out
    total = stack(totals)
    log_sum = stack(tops) + jnp.log(total)
    scaled = outs[...] * (1.0 / total)
    pieces = []
    rest = log_sum
    for part in range(3):
        pieces.append(rest.astype(BF).astype(F32))
        rest = rest - pieces[-1]
    for tile in tiles:
        rows = tile.stop - tile.start
        lane = lax.broadcasted_iota(jnp.int32, (rows, LANES), 1)
        attended = jnp.zeros((rows, width), F32)
        extra = jnp.zeros((rows, LANES), F32)
        for h in range(heads):
            first = tile.start * heads + h * rows
            cut = slice(first, first + rows)
            attended = jnp.where(masks[h][:rows], scaled[cut], attended)
            for part in range(3):
                extra = jnp.where(lane == part * heads + h, pieces[part][cut], extra)
        result[tile, :] = jnp.concatenate(
            [attended.astype(BF), extra.astype(BF)], axis=1
        )


def send_middle(attention, weights, keep_ref, send_ref, partial):
    partial[...] = dot(attention, weights[...])
    me = lax.axis_index("tensor")
    part = keep_ref.shape[1]
    for k in range(2 * keep_ref.shape[0]):
        ref = keep_ref if k % 2 == 0 else send_ref
        place = pl.ds(pl.multiple_of((me ^ k) * part, part), part)
        ref[k // 2] = partial[place, :].astype(BF)


def home_kernel(
    heads, bounds, packed, starts, spans, kv_ref, weights, result, keep_ref, send_ref, partial, outs
):
    attend_all(bounds, packed[...], starts, spans, kv_ref, result, heads, outs, Q_TILE)
    send_middle(result[:, : heads * HD], weights, keep_ref, send_ref, partial)


def far_kernel(heads, hop_count, bounds, *refs):
    arrived = jnp.concatenate([ref[...] for ref in refs[:hop_count]], axis=0)
    starts, spans, kv_ref, _ = refs[hop_count : hop_count + 4]
    *outs, result, state = refs[hop_count + 4 :]
    rows = arrived.shape[0] // hop_count
    attend_all(bounds, arrived, starts, spans, kv_ref, result, heads, state, rows)
    for k in range(hop_count):
        outs[k][...] = result[k * rows : (k + 1) * rows, :]


def far_out_kernel(heads, hop_count, slots, far_pick, home, *refs):
    backs = refs[:hop_count]
    weights, log_ref, keep_ref, send_ref, partial = refs[hop_count:]
    width = heads * HD
    far = jnp.concatenate([ref[...] for ref in backs], axis=0)
    placed = dot(one_hot(partial.shape[0], far_pick[...]), far[:, :width]).astype(BF)
    send_middle(placed, weights, keep_ref, send_ref, partial)
    extras = jnp.concatenate([home[:, width:], far[:, width:]], axis=0)
    extra = dot_tn(one_hot(extras.shape[0], slots[...]), extras)
    log_ref[...] = (
        extra + pltpu.roll(extra, LANES - heads, 1) + pltpu.roll(extra, LANES - 2 * heads, 1)
    )


def gate_kernel(piece_count, *refs):
    pieces = refs[:piece_count]
    gain, gate_up, inner_ref = refs[piece_count:]
    values = jnp.concatenate([piece[...] for piece in pieces], axis=0)
    normed = normalize(values, gain[...])
    gate = dot(normed, gate_up[0])
    upward = dot(normed, gate_up[1])
    inner_ref[...] = (gate / (1.0 + jnp.exp(-gate)) * upward).astype(BF)


def send_rows(partial, rows, keep_ref, send_ref):
    for k in range(partial.shape[0] // rows):
        ref = keep_ref if k % 2 == 0 else send_ref
        ref[k // 2] = partial[k * rows : (k + 1) * rows]


def down_first_kernel(rows, home, far, order, down, rest_ref, keep_ref, send_ref):
    both = jnp.concatenate([home[...], far[...]], axis=0)
    inner = dot_tn(one_hot(both.shape[0], order[...]), both).astype(BF)
    half = rest_ref.shape[0]
    rest_ref[...] = inner[:half]
    send_rows(dot(inner[half:], down[...]).astype(BF), rows, keep_ref, send_ref)


def down_second_kernel(rows, inner, down, keep_ref, send_ref):
    send_rows(dot(inner[...], down[...]).astype(BF), rows, keep_ref, send_ref)


def own_rows_kernel(order, *refs):
    pieces = refs[:-1]
    values = jnp.concatenate([piece[...] for piece in pieces], axis=0)
    rows = refs[-1].shape[0]
    chosen = dot_tn(one_hot(values.shape[0], order[...]), values)
    refs[-1][...] = chosen[:rows].astype(BF)


def update_kernel(hop_count, width, home_rows, far_rows, home, *refs):
    far = refs[:hop_count]
    kv_in, kv_out = refs[hop_count:]
    block = kv_in.shape[1]
    position = lax.broadcasted_iota(jnp.int32, (block, 1), 0) + pl.program_id(0) * block
    fresh = jnp.concatenate([home[:, width:]] + [ref[:, width:] for ref in far], axis=0)
    targets = jnp.concatenate([home_rows[...], far_rows[...]], axis=1)
    hit = jnp.where(position == targets, 1.0, 0.0)
    written = jnp.max(hit, axis=1, keepdims=True) > 0.0
    values = dot(hit.astype(BF), fresh).astype(BF)
    kv_out[0] = jnp.where(written, values[:, :width], kv_in[0])
    kv_out[1] = jnp.where(written, values[:, width:], kv_in[1])


def vmem(count):
    return [pl.BlockSpec(memory_space=pltpu.VMEM)] * count


def on_device(
    tokens,
    attn_gain,
    mlp_gain,
    project_in,
    project_out,
    gate_up,
    project_down,
    kv_cache,
    lengths,
    owners,
    cache_start,
):
    groups = lax.axis_size("dp")
    my_index = lax.axis_index("dp")
    tensor_count = lax.axis_size("tensor")
    me = lax.axis_index("tensor")
    rows, model_width = tokens.shape
    request_count = rows * tensor_count
    width = project_in.shape[2]
    heads = width // HD
    cache_rows = kv_cache.shape[1]
    home_count = round_up(request_count - request_count // 2, Q_TILE)
    hops = groups - 1
    capacity = (request_count // 2 + groups - 2) // (groups - 1)
    slot_rows = round_up(capacity, 16)
    far_count = hops * slot_rows
    shape = jax.ShapeDtypeStruct
    smem = pl.BlockSpec(memory_space=pltpu.SMEM)
    anywhere = pl.BlockSpec(memory_space=pl.ANY)

    def params(mebibytes):
        return pltpu.CompilerParams(vmem_limit_bytes=mebibytes * 1024 * 1024)

    def cost(flops, bytes_accessed, transcendentals=0):
        return pl.CostEstimate(
            flops=flops, bytes_accessed=bytes_accessed, transcendentals=transcendentals
        )

    ints = lambda *dims: shape(dims, jnp.int32)
    freqs = ROPE_BASE ** (-((jnp.arange(LANES) % (HD // 2)).astype(F32) * 2.0 / HD))
    plan = lambda: pl.pallas_call(
        functools.partial(
            plan_kernel,
            (groups, request_count, home_count, slot_rows, cache_rows, rows),
        ),
        out_shape=[
            ints(1, request_count),
            ints(1, request_count),
            ints(1, request_count),
            ints(1, far_count),
            shape((request_count, LANES), F32),
            shape((request_count, LANES), F32),
            ints(home_count, 1),
            ints(home_count, 1),
            ints(1, home_count),
            ints(2, home_count // Q_TILE),
            ints(far_count, 1),
            ints(far_count, 1),
            ints(1, far_count),
            ints(2, hops),
        ],
        in_specs=vmem(4),
        out_specs=vmem(9) + [smem] + vmem(3) + [smem],
        compiler_params=params(16),
        cost_estimate=cost(4 * 10**9, 10**6, 10**5),
        name="plan",
    )(lengths[None, :], owners[None, :], cache_start[None, :], freqs[None, :])
    pieces, planned = gather_tensor(tokens, plan)
    (
        slots,
        middle,
        own_order,
        far_pick,
        cosine,
        sine,
        home_start,
        home_span,
        home_write,
        home_bounds,
        far_start,
        far_span,
        far_write,
        far_bounds,
    ) = planned

    part = rows // 2
    middle_count = request_count // 2
    half_count = tensor_count // 2
    packed_outs = pl.pallas_call(
        functools.partial(qkv_kernel, tensor_count, home_count, slot_rows, hops),
        out_shape=[shape((home_count, 3 * width), BF)]
        + [shape((slot_rows, 3 * width), BF)] * hops
        + [shape((part, model_width), BF)] * 2,
        in_specs=vmem(tensor_count + 6),
        out_specs=vmem(3 + hops),
        scratch_shapes=[pltpu.VMEM((request_count, model_width), BF)] * 2,
        compiler_params=params(16),
        name="qkv",
    )(*pieces, attn_gain[None, :], project_in, cosine, sine, slots, middle)
    home_packed = packed_outs[0]
    token_home, token_far = packed_outs[1 + hops :]
    arrived = [swap(packed_outs[k], "dp", k) for k in range(1, groups)]

    out_width = width + LANES
    sums = [shape((half_count, part, model_width), BF)] * 2
    partial_scratch = pltpu.VMEM((middle_count, model_width), F32)
    home_att, keep, send = pl.pallas_call(
        functools.partial(home_kernel, heads),
        out_shape=[shape((home_count, out_width), BF)] + sums,
        in_specs=[smem] + vmem(5),
        out_specs=vmem(3),
        scratch_shapes=[partial_scratch, pltpu.VMEM((home_count * heads, width), F32)],
        compiler_params=params(16),
        cost_estimate=cost(2 * 10**9, 4 * 2**20, 10**6),
        name="home_attention",
    )(home_bounds, home_packed, home_start, home_span, kv_cache, project_out)
    (keep, send), arrived = lax.optimization_barrier(((keep, send), arrived))
    home_sums = reduce_chips(keep, send, 0)
    far_outs = pl.pallas_call(
        functools.partial(far_kernel, heads, hops),
        out_shape=[shape((slot_rows, out_width), BF)] * hops,
        in_specs=[smem] + vmem(hops + 3) + [anywhere],
        out_specs=vmem(hops),
        scratch_shapes=[
            pltpu.VMEM((far_count, out_width), BF),
            pltpu.VMEM((far_count * heads, width), F32),
        ],
        compiler_params=params(16),
        cost_estimate=cost(2 * 10**9, 4 * 2**20, 10**6),
        name="far_attention",
    )(far_bounds, *arrived, far_start, far_span, kv_cache, home_att)
    backs = [swap(far_outs[k - 1], "dp", k) for k in range(1, groups)]

    block = 512
    kv_spec = pl.BlockSpec((2, block, width), lambda i: (0, i, 0))
    fixed = lambda array: pl.BlockSpec(array.shape, lambda i: (0,) * array.ndim)
    kv_updated = pl.pallas_call(
        functools.partial(update_kernel, hops, width),
        grid=(cache_rows // block,),
        out_shape=shape(kv_cache.shape, BF),
        in_specs=[fixed(home_write), fixed(far_write), fixed(home_packed)]
        + [fixed(a) for a in arrived]
        + [kv_spec],
        out_specs=kv_spec,
        compiler_params=params(16),
        cost_estimate=cost(2 * 10**9, 8 * 2**20),
        name="cache_update",
    )(home_write, far_write, home_packed, *arrived, kv_cache)

    def add_up(base, sums):
        return (base.astype(F32) + sum(piece.astype(F32) for piece in sums)).astype(BF)

    hidden = gate_up.shape[2]
    gate = lambda pieces, name: pl.pallas_call(
        functools.partial(gate_kernel, tensor_count),
        out_shape=shape((middle_count, hidden), BF),
        in_specs=vmem(tensor_count + 2),
        out_specs=vmem(1)[0],
        compiler_params=params(16),
        cost_estimate=cost(2 * 10**9, 8 * 2**20),
        name=name,
    )(*pieces, mlp_gain[None, :], gate_up)
    backs, home_sums = lax.optimization_barrier((backs, home_sums))
    home_far_chips = gather_chips(add_up(token_home, home_sums))

    log_sum, keep, send = pl.pallas_call(
        functools.partial(far_out_kernel, heads, hops),
        out_shape=[shape((request_count, LANES), F32)] + sums,
        in_specs=vmem(4 + hops),
        out_specs=vmem(3),
        scratch_shapes=[partial_scratch],
        compiler_params=params(16),
        name="project_out_far",
    )(slots, far_pick, home_att, *backs, project_out)
    log_sum_exp = log_sum[:, :heads]
    far_sums = reduce_chips(keep, send, 0)
    home_pieces = gather_cores(home_far_chips)
    far_pieces, home_inner = gather_tensor(
        add_up(token_far, far_sums), lambda: gate(home_pieces, "gate_up_home")
    )
    far_inner = gate(far_pieces, "gate_up_far")

    near = half_count // 2
    quarters = [shape((near, rows, model_width), BF)] * 2
    rest, keep, send = pl.pallas_call(
        functools.partial(down_first_kernel, rows),
        out_shape=[shape((middle_count, hidden), BF)] + quarters,
        in_specs=vmem(4),
        out_specs=vmem(3),
        compiler_params=params(16),
        name="down_first",
    )(home_inner, far_inner, own_order, project_down)
    down_sums = reduce_chips(keep, send, near)
    keep, send = pl.pallas_call(
        functools.partial(down_second_kernel, rows),
        out_shape=quarters,
        in_specs=vmem(2),
        out_specs=vmem(2),
        compiler_params=params(16),
        name="down_second",
    )(rest, project_down)
    down_sums += reduce_chips(keep, send, 0)
    resid = pl.pallas_call(
        own_rows_kernel,
        out_shape=shape(tokens.shape, BF),
        in_specs=vmem(1 + 2 * tensor_count),
        out_specs=vmem(1)[0],
        compiler_params=params(16),
        name="own_rows",
    )(own_order, *home_pieces, *far_pieces)
    hidden_states = add_up(resid, down_sums)
    return (hidden_states, log_sum_exp, kv_updated)


def solution(mesh):
    placed = (
        P(("dp", "tensor"), None),
        P(),
        P(),
        P(None, None, "tensor"),
        P("tensor", None),
        P(None, None, "tensor"),
        P("tensor", None),
        P(None, "dp", "tensor"),
        P(),
        P(),
        P(),
    )
    return jax.shard_map(
        on_device,
        mesh=mesh,
        in_specs=placed,
        out_specs=(P(("dp", "tensor"), None), P("dp", "tensor"), P(None, "dp", "tensor")),
        check_vma=False,
    )
```
